256 devices in a mesh: seq: 16 (over x_hi, y, core), fsdp: 16 (over z, x_lo).
Axes of the slice: x: 4 (x_hi: 2, x_lo: 2; x = x_hi * 2 + x_lo), y: 4, z: 8, core: 2. Of those that a mesh axis runs over, the one named last changes fastest.
Arguments:
- query_states: bfloat16 [4096, 4096], P('seq', 'fsdp'), may hold values from -24 to 24
- key_states: bfloat16 [4096, 4096], P('seq', 'fsdp'), may hold values from -6 to 6
- value_states: bfloat16 [4096, 4096], P('seq', 'fsdp'), may hold values from -6 to 6
- positions: int32 [4096], P('seq'), may hold values from 0 to 4095, as said below
- out_weight: bfloat16 [4096, 5120], P('fsdp', 'seq'), may hold values from -1 to 1
- cotangent: bfloat16 [4096, 5120], P('seq', 'fsdp'), may hold values from -0.59765625 to 0.59765625
Outputs:
- attn_output: float32 [4096, 5120], P('seq', 'fsdp')
- grad_queries: float32 [4096, 4096], P('seq', 'fsdp')
- grad_keys: float32 [4096, 4096], P('seq', 'fsdp')
- grad_values: float32 [4096, 4096], P('seq', 'fsdp')
- grad_weight: float32 [4096, 5120], P('fsdp', 'seq')
The draws below stay inside these ranges and needn't reach their ends.
Inputs may be any that keep to these rules, and one draw needn't show every extreme that they name: A permutation of 0 to 4095; each aligned block of 256 rows holds, in increasing order, the positions of one residue class modulo 4096 // 256.
All inputs are finite; a program needn't handle non-finite values.
Results may differ from the reference program's by a relative error of at most 0.02.
Values may be sent and summed in bfloat16 or wider, within the bound.
A program may use at most 128 MiB of HBM per device.

```python
import jax
import jax.numpy as jnp
from jax import lax

D = 5120
HEADS = 32
HEAD_DIM = 128
TOK_DEV = 256
SEQ_LEN = 4096
N_FSDP = 16


def drawn_pair(key):
    base = jax.random.fold_in(key, 11)
    key_query, key_key = jax.random.split(base, 2)
    shape = (SEQ_LEN, HEADS, HEAD_DIM)
    query_draw = 1.2 * jax.random.truncated_normal(key_query, -5.0, 5.0, shape, jnp.float32)
    key_draw = 1.2 * jax.random.truncated_normal(key_key, -5.0, 5.0, shape, jnp.float32)
    return (query_draw.reshape(SEQ_LEN, HEADS * HEAD_DIM), key_draw.reshape(SEQ_LEN, HEADS * HEAD_DIM))


def draw_query_states(key, part):
    return drawn_pair(key)[0].astype(jnp.bfloat16)


def draw_key_states(key, part):
    return drawn_pair(key)[1].astype(jnp.bfloat16)


def draw_positions(key, part):
    blocks = SEQ_LEN // TOK_DEV
    residues = jax.random.permutation(jax.random.fold_in(key, 23), blocks).astype(jnp.int32)
    row_index = jnp.arange(SEQ_LEN, dtype=jnp.int32)
    block_index = row_index // TOK_DEV
    local_row = row_index % TOK_DEV
    return (local_row * blocks + residues[block_index]).astype(jnp.int32)


def raised(values, key, source, target, parts, factor):
    owner, partner = [(jnp.arange(values.shape[position]) // (values.shape[position] // parts)).reshape([-1 if axis == position else 1 for axis in range(values.ndim)]) for position in (source, target)]
    chosen = jax.random.permutation(key, parts)[partner]
    strong = (owner == chosen) | (owner == (partner + parts // 2) % parts)
    return jnp.where(strong, factor * values, values)


def levels(own_key, extent, pieces, smallest, high):
    factor_of, own = 1.0, jax.random.fold_in(own_key, 6)
    for axis_at, parts in pieces:
        steps = jnp.exp(jax.random.uniform(jax.random.fold_in(own, axis_at), (parts,), jnp.float32, smallest / len(pieces), high / len(pieces)))
        factor_of = factor_of * jnp.repeat(steps, extent[axis_at] // parts).reshape([-1 if axis == axis_at else 1 for axis in range(len(extent))])
    return factor_of


def noise(own_key, dims, spread, reach, cuts=(), kind=jnp.bfloat16):
    drawn = jax.random.normal(own_key, dims, jnp.float32) * spread
    if len(cuts) > 0:
        drawn = levels(own_key, dims, cuts, -0.22, 0.18) * drawn
    return jnp.clip(drawn, min=-reach, max=reach).astype(kind)


def bell_draw_with(own_key, extent, deviation, reach, shards, heavy, kind=jnp.bfloat16):
    entries = deviation * jax.random.normal(own_key, extent, jnp.float32)
    if shards:
        entries = entries * levels(own_key, extent, shards, -0.22, 0.18)
    return jnp.clip(raised(entries, jax.random.fold_in(own_key, 3), *heavy), -reach, reach).astype(kind)


def setup_inputs(seed: int = 0) -> dict:
    keys = jax.random.split(jax.random.key(seed), 7)
    return {
        "query_states": draw_query_states(jax.random.fold_in(keys[6], 71), 0),
        "key_states": draw_key_states(jax.random.fold_in(keys[6], 71), 0),
        "value_states": noise(keys[2], (SEQ_LEN, HEADS * HEAD_DIM), 1.0, 6.0, ((0, 16), (1, 16))),
        "positions": draw_positions(jax.random.fold_in(keys[6], 71), 0),
        "out_weight": bell_draw_with(keys[4], (HEADS * HEAD_DIM, D), (HEADS * HEAD_DIM // 64) ** -0.5, 1.0, ((0, 16), (1, 16)), (0, 1, 16, 2.0)),
        "cotangent": bell_draw_with(keys[5], (SEQ_LEN, D), 0.1, 0.59765625, ((0, 16), (1, 16)), (0, 1, 16, 2.0)),
    }


blocked = -1e30


def split_heads(matrix):
    return matrix.reshape(matrix.shape[0], HEADS, HEAD_DIM).transpose(1, 0, 2)


def join_heads(stacked):
    return stacked.transpose(1, 0, 2).reshape(stacked.shape[1], HEADS * HEAD_DIM)


def reference(query_states, key_states, value_states, positions, out_weight, cotangent):
    score_scale = HEAD_DIM ** -0.5
    visible = positions[None, :] <= positions[:, None]

    def head_scores(query_rows, key_rows):
        raw = jnp.dot(query_rows, key_rows.T, preferred_element_type=jnp.float32) * score_scale
        return jnp.where(visible, raw, blocked)

    def forward_head(operands):
        query_rows, key_rows, value_rows = operands
        scores = head_scores(query_rows, key_rows)
        row_max = jnp.max(scores, axis=1)
        log_total = row_max + jnp.log(jnp.sum(jnp.exp(scores - row_max[:, None]), axis=1))
        weights = jnp.exp(scores - log_total[:, None]).astype(jnp.bfloat16)
        output_rows = jnp.dot(weights, value_rows, preferred_element_type=jnp.float32).astype(jnp.bfloat16)
        return log_total, output_rows

    query_heads = split_heads(query_states)
    key_heads = split_heads(key_states)
    value_heads = split_heads(value_states)
    log_totals, attended_heads = lax.map(forward_head, (query_heads, key_heads, value_heads))
    attended = join_heads(attended_heads)

    group_width = (HEADS // N_FSDP) * HEAD_DIM

    def add_group(running, group_index):
        columns = lax.dynamic_slice_in_dim(attended, group_index * group_width, group_width, 1)
        weight_rows = lax.dynamic_slice_in_dim(out_weight, group_index * group_width, group_width, 0)
        partial_sum = jnp.dot(columns, weight_rows, preferred_element_type=jnp.float32).astype(jnp.bfloat16)
        partial_sum = lax.optimization_barrier(partial_sum)
        return running + partial_sum.astype(jnp.float32), None

    summed, _ = lax.scan(add_group, jnp.zeros((SEQ_LEN, D), jnp.float32), jnp.arange(N_FSDP, dtype=jnp.int32))
    attn_output = summed

    grad_attended = jnp.dot(cotangent, out_weight.T, preferred_element_type=jnp.float32).astype(jnp.bfloat16)
    grad_weight = jnp.dot(attended.T, cotangent, preferred_element_type=jnp.float32)

    def backward_head(operands):
        query_rows, key_rows, value_rows, grad_rows, output_rows, log_total = operands
        row_delta = jnp.sum(grad_rows.astype(jnp.float32) * output_rows.astype(jnp.float32), axis=1)
        scores = head_scores(query_rows, key_rows)
        probs = jnp.exp(scores - log_total[:, None])
        grad_probs = jnp.dot(grad_rows, value_rows.T, preferred_element_type=jnp.float32)
        grad_scores = (probs * (grad_probs - row_delta[:, None])).astype(jnp.bfloat16)
        grad_query = jnp.dot(grad_scores, key_rows, preferred_element_type=jnp.float32) * score_scale
        grad_key = jnp.dot(grad_scores.T, query_rows, preferred_element_type=jnp.float32) * score_scale
        grad_value = jnp.dot(probs.astype(jnp.bfloat16).T, grad_rows, preferred_element_type=jnp.float32)
        return grad_query, grad_key, grad_value

    grads = lax.map(backward_head, (query_heads, key_heads, value_heads, split_heads(grad_attended), attended_heads, log_totals))
    return attn_output, join_heads(grads[0]), join_heads(grads[1]), join_heads(grads[2]), grad_weight
```

```python
import math

import jax
import jax.numpy as jnp
from jax import lax
from jax.experimental import pallas as pl
from jax.experimental.pallas import tpu as pltpu
from jax.sharding import PartitionSpec as P

HEAD_DIM = 128
TOKENS = 256
HALF = 128
COLS = 320
FEATS = 256
MESH = pl.DeviceIdType.MESH
BF16 = jnp.bfloat16
F32 = jnp.float32
SCALE = HEAD_DIM ** (-0.5)
SCALE_LOG2 = SCALE * math.log2(math.e)
BLOCKED = -1e30
SEMS = 80


def mm(a, b):
    return jnp.dot(a, b, preferred_element_type=F32)


def mm_nt(a, b):
    return lax.dot_general(a, b, (((1,), (1,)), ((), ())), preferred_element_type=F32)


def mm_tn(a, b):
    return lax.dot_general(a, b, (((0,), (0,)), ((), ())), preferred_element_type=F32)


def kernel(
    q_ref, k_ref, v_ref, res_ref, w_ref, ct_ref,
    out_ref, dq_ref, dk_ref, dv_ref, gw_ref,
    kvr, kvp, qt, qp, wt, cot,
    m_ref, l_ref, acc, att_t, att, att_full,
    pga, pga_in, grad_t, grad, delta,
    out_send, out_rin, out_lin, out_pair_ici, out_pair_core,
    gw_send, gw_rin2, gw_lin2, gw_rin, gw_lin, gw_x, gw_own,
    df, d_send, d_rin2, d_lin2, d_rin, d_lin, d_x, fin, fin_in,
    dq_t, dq_b, dq_in,
    ss, rs,
):
    seq = lax.axis_index("seq")
    fsdp = lax.axis_index("fsdp")
    xh, y, c = seq // 8, (seq // 2) % 4, seq % 2
    z, xl = fsdp // 2, fsdp % 2
    p = 1 - c
    same = c == xl

    def dev(xh_, y_, c_, z_, xl_):
        return (xh_ * 8 + y_ * 2 + c_, z_ * 2 + xl_)

    yr, yl, y2 = (y + 1) % 4, (y + 3) % 4, (y + 2) % 4
    zr, zl = (z + 1) % 8, (z + 7) % 8
    core_peer = dev(xh, y, p, z, xl)
    xh_peer = dev(1 - xh, y, c, z, xl)
    y_right, y_left = dev(xh, yr, c, z, xl), dev(xh, yl, c, z, xl)
    z_right, z_left = dev(xh, y, c, zr, xl), dev(xh, y, c, zl, xl)
    xl_peers = [dev(xh, y, h, z, 1 - xl) for h in range(2)]
    xl_owner = dev(xh, y, xl, z, 1 - xl)

    used = [0]
    sent = []

    def take(count=1):
        first = used[0]
        used[0] += count
        return first

    def copy(src, dst, to):
        i = take()
        d = pltpu.make_async_remote_copy(
            src_ref=src, dst_ref=dst, send_sem=ss.at[i], recv_sem=rs.at[i],
            device_id=to, device_id_type=MESH,
        )
        d.start()
        sent.append(d)
        return d

    barrier = pltpu.get_barrier_semaphore()
    peers = [core_peer, xh_peer, y_right, y_left, z_right, z_left] + xl_peers
    for peer in peers:
        pl.semaphore_signal(barrier, inc=1, device_id=peer, device_id_type=MESH)
    pl.semaphore_wait(barrier, len(peers))

    sem_ici, sem_core = take(2), take()
    cot_ici = pltpu.make_async_remote_copy(
        src_ref=ct_ref, dst_ref=cot.at[z, c], send_sem=ss.at[sem_ici], recv_sem=rs.at[sem_ici + c],
        device_id=xl_owner, device_id_type=MESH,
    )
    cot_ici.start()
    sent.append(cot_ici)
    cot_core = pltpu.make_async_remote_copy(
        src_ref=ct_ref, dst_ref=cot.at[z, c], send_sem=ss.at[sem_core], recv_sem=rs.at[sem_core],
        device_id=core_peer, device_id_type=MESH,
    )

    @pl.when(jnp.logical_not(same))
    def _():
        cot_core.start()

    first = c == 0
    own = y * 4 + xh * 2
    for part, ref in ((0, k_ref), (1, v_ref)):
        lo, hi = ref[:, :HEAD_DIM], ref[:, HEAD_DIM:]
        rows = pl.ds(part * TOKENS, TOKENS)
        kvp[rows, :] = jnp.where(first, hi, lo)
        kvr[own + c, rows, :] = jnp.where(first, lo, hi)
    kvp[pl.ds(2 * TOKENS, 16), :] = res_ref[...]
    kvr[own + c, pl.ds(2 * TOKENS, 16), :] = res_ref[...]
    kv_core = copy(kvp, kvr.at[own + c], core_peer)
    for i in range(2):
        rows = pl.ds(i * HALF, HALF)
        lo, hi = q_ref[rows, :HEAD_DIM], q_ref[rows, HEAD_DIM:]
        qp[i] = jnp.where(first, hi, lo)
        qt[i, c] = jnp.where(first, lo, hi)
    q_core = copy(qp, qt.at[:, c], core_peer)

    w_own = y * 2 + xh
    wt[w_own] = w_ref[...]

    @pl.when(same)
    def _():
        cot[z, c] = ct_ref[...]

    acc[...] = jnp.zeros_like(acc)
    l_ref[...] = jnp.zeros_like(l_ref)
    m_ref[...] = jnp.full_like(m_ref, BLOCKED)

    kv_core.wait_recv()

    def kv_direct(x):
        block = kvr.at[pl.ds(y * 4 + x * 2, 2)]
        return copy(block, block, y_right), copy(block, block, y_left)

    def kv_forward(x):
        low, high = kvr.at[yl * 4 + x * 2], kvr.at[yr * 4 + x * 2 + 1]
        return copy(low, low, y_right), copy(high, high, y_left)

    def w_direct(x):
        block = wt.at[y * 2 + x]
        return copy(block, block, y_right), copy(block, block, y_left)

    def w_forward(x):
        low, high = wt.at[yl * 2 + x, pl.ds(0, 160)], wt.at[yr * 2 + x, pl.ds(160, 160)]
        return copy(low, low, y_right), copy(high, high, y_left)

    def both_recv(pair):
        pair[0].wait_recv()
        pair[1].wait_recv()

    kv_xh = copy(kvr.at[pl.ds(own, 2)], kvr.at[pl.ds(own, 2)], xh_peer)
    kv_mine = kv_direct(xh)

    @pl.when(same)
    def _():
        cot_core.wait_recv()

    @pl.when(jnp.logical_not(same))
    def _():
        for h in range(2):
            pltpu.make_async_remote_copy(
                src_ref=ct_ref, dst_ref=cot.at[z, h], send_sem=ss.at[sem_ici],
                recv_sem=rs.at[sem_ici + h], device_id=xl_owner, device_id_type=MESH,
            ).wait_recv()

    def z_pair(right_slot, left_slot):
        a, b = cot.at[right_slot], cot.at[left_slot]
        return copy(a, a, z_right), copy(b, b, z_left)

    z_one = z_pair(z, z)
    w_xh = copy(wt.at[w_own], wt.at[w_own], xh_peer)
    q_core.wait_recv()

    kv_xh.wait_recv()
    kv_other = kv_direct(1 - xh)
    both_recv(kv_mine)
    kv_mine_far = kv_forward(xh)
    both_recv(z_one)
    z_two = z_pair((z + 7) % 8, (z + 1) % 8)
    w_mine = w_direct(xh)

    ahead = (
        lax.broadcasted_iota(jnp.int32, (1, HALF, TOKENS), 2) % HALF
        - lax.broadcasted_iota(jnp.int32, (1, HALF, TOKENS), 1)
    )

    def residue_rows(slot, count):
        return kvr[pl.ds(slot, count), pl.ds(2 * TOKENS, 16), :].astype(F32)[:, 0:1, :]

    query_res = residue_rows(own, 2)
    query_res = jnp.concatenate([query_res[0:1], query_res[1:2]], axis=2)

    def tile_scores(yy, t, qi, ki):
        key_res = residue_rows(yy * 4, 4)
        key_res = jnp.concatenate([key_res, key_res], axis=2)
        bound = jnp.where(key_res <= query_res, 0, 1) - jnp.where(qi > ki, 4 * HALF, 0)
        rows = pl.multiple_of(ki * HALF, HALF)
        keys = kvr[pl.ds(yy * 4, 4), pl.ds(rows, HALF), :].reshape(4 * HALF, HEAD_DIM)
        values = kvr[pl.ds(yy * 4, 4), pl.ds(TOKENS + rows, HALF), :].reshape(4 * HALF, HEAD_DIM)
        queries = qt[qi].reshape(TOKENS, HEAD_DIM)
        scores = mm_nt(keys, queries) * SCALE_LOG2
        seen = ahead >= bound
        scores = jnp.where(seen, scores.reshape(4, HALF, TOKENS), BLOCKED)
        return scores.reshape(4 * HALF, TOKENS), keys, values, queries

    def forward(yy):
        def tile(t, carry):
            qi, ki = (t + 1) // 2, t // 2
            scores, _, values, _ = tile_scores(yy, t, qi, ki)
            old = m_ref[qi]
            new = jnp.maximum(old, jnp.max(scores, axis=0, keepdims=True))
            probs = jnp.exp2(scores - new)
            shrink = jnp.exp2(old - new)
            m_ref[qi] = new
            l_ref[qi] = l_ref[qi] * shrink + jnp.sum(probs, axis=0, keepdims=True)
            acc[qi] = acc[qi] * shrink + mm_tn(values, probs.astype(BF16))
            return carry

        lax.fori_loop(0, 3, tile, 0)

    forward(y)
    w_xh.wait_recv()
    w_other = w_direct(1 - xh)
    both_recv(kv_other)
    kv_other_far = kv_forward(1 - xh)
    both_recv(z_two)
    z_three = z_pair((z + 6) % 8, (z + 2) % 8)
    forward(yl)
    forward(yr)
    both_recv(w_mine)
    w_mine_far = w_forward(xh)
    both_recv(z_three)
    z_four = (
        copy(cot.at[(z + 5) % 8, 0], cot.at[(z + 5) % 8, 0], z_right),
        copy(cot.at[(z + 3) % 8, 1], cot.at[(z + 3) % 8, 1], z_left),
    )
    both_recv(w_other)
    w_other_far = w_forward(1 - xh)
    both_recv(kv_mine_far)
    both_recv(kv_other_far)
    forward(y2)

    for qi in range(2):
        total = l_ref[qi]
        rows = (acc[qi] / total).astype(BF16)
        att_t[qi] = rows
        m_ref[qi] = m_ref[qi] + jnp.log2(total)
        wide = rows.astype(F32)
        for h in range(2):
            att[c, h, pl.ds(qi * HALF, HALF), :] = wide[:, h * HALF:(h + 1) * HALF].T.astype(BF16)
    att_core = copy(att.at[c], att.at[c], core_peer)
    both_recv(w_mine_far)
    both_recv(w_other_far)
    att_core.wait_recv()
    for h in range(2):
        att_full[h] = jnp.concatenate([att[0, h], att[1, h]], axis=1)

    def w_block(i):
        return wt[(i % 4) * 2 + i // 4]

    def out_term(i, h):
        return mm_nt(w_block(i), att_full[h])

    def out_step(step, got):
        to_right, to_left = (z + 4 - step) % 8, (z + 4 + step) % 8
        if step == 0:
            out_send[0, 0, 0] = out_term(to_right, 0).astype(BF16)
            out_send[1, 0, 1] = out_term(to_left, 1).astype(BF16)
            return (
                copy(out_send.at[0, 0, 0], out_rin.at[0, 0], z_right),
                copy(out_send.at[1, 0, 1], out_lin.at[0, 1], z_left),
            )
        both_recv(got)
        for side, target, arrived in ((0, to_right, out_rin), (1, to_left, out_lin)):
            for h in range(2):
                term = out_term(target, h)
                if step > 1 or h == side:
                    term = term + arrived[step - 1, h].astype(F32)
                out_send[side, step, h] = term.astype(BF16)
        return (
            copy(out_send.at[0, step], out_rin.at[step], z_right),
            copy(out_send.at[1, step], out_lin.at[step], z_left),
        )

    out_0 = out_step(0, None)
    both_recv(z_four)

    pga[...] = jnp.zeros_like(pga)

    def width_step(i, carry):
        weight = w_block(i)
        for h in range(2):
            term = mm_tn(weight, cot[i, h])
            pga[0, h] += term[:HEAD_DIM]
            pga[1, h] += term[HEAD_DIM:]
        return carry

    lax.fori_loop(0, 8, width_step, 0)
    pga_core = copy(pga.at[p], pga_in, core_peer)

    def gw_term(x, yy):
        i = x * 4 + yy
        return mm(cot[i, 0], att_full[0]) + mm(cot[i, 1], att_full[1])

    for x in range(2):
        gw_send[0, x] = gw_term(x, y2).astype(BF16)
    gw_far = (copy(gw_send.at[0, 0], gw_rin2, y_right), copy(gw_send.at[0, 1], gw_lin2, y_left))

    pga_core.wait_recv()
    for h in range(2):
        rows = (pga[c, h] + pga_in[h]).astype(BF16)
        for qi in range(2):
            grad_t[qi, :, h * HALF:(h + 1) * HALF] = rows[:, qi * HALF:(qi + 1) * HALF]
    for qi in range(2):
        wide = grad_t[qi].astype(F32)
        delta[qi] = jnp.sum(wide * att_t[qi].astype(F32), axis=0, keepdims=True)
        grad[qi] = wide.T.astype(BF16)
    dq_t[...] = jnp.zeros_like(dq_t)

    def backward(yy):
        df[...] = jnp.zeros_like(df)

        def tile(t, carry):
            qi, ki = (t + 1) // 2, t // 2
            scores, keys, values, queries = tile_scores(yy, t, qi, ki)
            probs = jnp.exp2(scores - m_ref[qi])
            grad_probs = mm(values, grad_t[qi])
            grad_scores = (probs * (grad_probs - delta[qi])).astype(BF16)
            rows = pl.ds(pl.multiple_of(ki * HALF, HALF), HALF)
            grad_keys = mm(grad_scores, queries).reshape(4, HALF, HEAD_DIM)
            grad_values = mm(probs.astype(BF16), grad[qi]).reshape(4, HALF, HEAD_DIM)
            df[:, 0, rows, :] += grad_keys
            df[:, 1, rows, :] += grad_values
            dq_t[qi] += mm_tn(keys, grad_scores)
            return carry

        lax.fori_loop(0, 3, tile, 0)

    backward(y2)
    for x in range(2):
        d_send[0, pl.ds(2 * x, 2)] = df[pl.ds(2 * x, 2)].astype(BF16)
    d_far = (
        copy(d_send.at[0, pl.ds(0, 2)], d_rin2, y_right),
        copy(d_send.at[0, pl.ds(2, 2)], d_lin2, y_left),
    )
    out_1 = out_step(1, out_0)

    both_recv(gw_far)
    gw_send[1, 0] = (gw_term(0, yr) + gw_rin2[...].astype(F32)).astype(BF16)
    gw_send[1, 1] = gw_term(1, yr).astype(BF16)
    gw_send[2, 0] = gw_term(0, yl).astype(BF16)
    gw_send[2, 1] = (gw_term(1, yl) + gw_lin2[...].astype(F32)).astype(BF16)

    backward(yr)
    both_recv(d_far)
    d_send[1, pl.ds(0, 2)] = (df[pl.ds(0, 2)] + d_rin2[...].astype(F32)).astype(BF16)
    d_send[1, pl.ds(2, 2)] = df[pl.ds(2, 2)].astype(BF16)
    d_right = copy(d_send.at[1], d_rin, y_right)
    backward(yl)
    d_send[2, pl.ds(0, 2)] = df[pl.ds(0, 2)].astype(BF16)
    d_send[2, pl.ds(2, 2)] = (df[pl.ds(2, 2)] + d_lin2[...].astype(F32)).astype(BF16)
    d_left = copy(d_send.at[2], d_lin, y_left)
    gw_near = (copy(gw_send.at[1], gw_rin, y_right), copy(gw_send.at[2], gw_lin, y_left))
    out_2 = out_step(2, out_1)

    backward(y)
    for qi in range(2):
        for h in range(2):
            dq_b[h, pl.ds(qi * HALF, HALF), :] = dq_t[qi, :, h * HALF:(h + 1) * HALF].T * SCALE
    dq_core = copy(dq_b.at[p], dq_in, core_peer)
    out_3 = out_step(3, out_2)

    d_right.wait_recv()
    d_left.wait_recv()
    d_send[3, pl.ds(0, 2)] = (
        df[pl.ds(2 * (1 - xh), 2)]
        + d_rin[pl.ds(2 * (1 - xh), 2)].astype(F32)
        + d_lin[pl.ds(2 * (1 - xh), 2)].astype(F32)
    ).astype(BF16)
    d_over = copy(d_send.at[3, pl.ds(0, 2)], d_x, xh_peer)

    both_recv(gw_near)
    for x in range(2):
        gw_own[x] = gw_term(x, y) + gw_rin[x].astype(F32) + gw_lin[x].astype(F32)
    gw_send[3, 0] = gw_own[1 - xh].astype(BF16)
    gw_over = copy(gw_send.at[3, 0], gw_x, xh_peer)

    def place(ref, mine, theirs):
        ref[:, :HEAD_DIM] = jnp.where(first, mine, theirs)
        ref[:, HEAD_DIM:] = jnp.where(first, theirs, mine)

    dq_core.wait_recv()
    place(dq_ref, dq_b[c], dq_in[...])

    d_over.wait_recv()
    for part in range(2):
        total = (
            df[pl.ds(2 * xh, 2), part]
            + d_rin[pl.ds(2 * xh, 2), part].astype(F32)
            + d_lin[pl.ds(2 * xh, 2), part].astype(F32)
            + d_x[:, part].astype(F32)
        )
        fin[:, part] = total * SCALE if part == 0 else total
    fin_core = copy(fin.at[p], fin_in, core_peer)

    both_recv(out_3)
    for h in range(2):
        term = out_term(z, h) + out_rin[3, h].astype(F32) + out_lin[3, h].astype(F32)
        out_send[0, 4, h] = term.astype(BF16)
    pair_ici, pair_core = take(2), take()
    to_peers = [
        pltpu.make_async_remote_copy(
            src_ref=out_send.at[0, 4, h], dst_ref=out_pair_ici, send_sem=ss.at[pair_ici + h],
            recv_sem=rs.at[pair_ici], device_id=xl_peers[h], device_id_type=MESH,
        )
        for h in range(2)
    ]
    to_core = pltpu.make_async_remote_copy(
        src_ref=out_send.at[0, 4, p], dst_ref=out_pair_core, send_sem=ss.at[pair_core],
        recv_sem=rs.at[pair_core], device_id=core_peer, device_id_type=MESH,
    )

    @pl.when(same)
    def _():
        to_core.start()

    @pl.when(jnp.logical_not(same))
    def _():
        to_peers[0].start()
        to_peers[1].start()

    gw_over.wait_recv()
    gw_ref[...] = gw_own[xh] + gw_x[...].astype(F32)

    fin_core.wait_recv()
    place(dk_ref, fin[c, 0], fin_in[0])
    place(dv_ref, fin[c, 1], fin_in[1])

    to_peers[0].wait_recv()

    @pl.when(same)
    def _():
        out_ref[...] = out_send[0, 4, c].astype(F32) + out_pair_ici[...].astype(F32)
        to_core.wait_send()

    @pl.when(jnp.logical_not(same))
    def _():
        to_core.wait_recv()
        out_ref[...] = out_pair_core[...].astype(F32) + out_pair_ici[...].astype(F32)
        to_peers[0].wait_send()
        to_peers[1].wait_send()
        cot_core.wait_send()

    for d in sent:
        d.wait_send()
    assert used[0] <= SEMS, used[0]


def fused(q, k, v, res, w, ct):
    vm = pltpu.VMEM
    scratch = [
        vm((16, 2 * TOKENS + 16, HEAD_DIM), BF16),
        vm((2 * TOKENS + 16, HEAD_DIM), BF16),
        vm((2, 2, HALF, HEAD_DIM), BF16),
        vm((2, HALF, HEAD_DIM), BF16),
        vm((8, COLS, FEATS), BF16),
        vm((8, 2, COLS, TOKENS), BF16),
        vm((2, 1, TOKENS), F32),
        vm((2, 1, TOKENS), F32),
        vm((2, HEAD_DIM, TOKENS), F32),
        vm((2, HEAD_DIM, TOKENS), BF16),
        vm((2, 2, TOKENS, HEAD_DIM), BF16),
        vm((2, TOKENS, FEATS), BF16),
        vm((2, 2, HEAD_DIM, TOKENS), F32),
        vm((2, HEAD_DIM, TOKENS), F32),
        vm((2, HEAD_DIM, TOKENS), BF16),
        vm((2, TOKENS, HEAD_DIM), BF16),
        vm((2, 1, TOKENS), F32),
        vm((2, 5, 2, COLS, TOKENS), BF16),
        vm((4, 2, COLS, TOKENS), BF16),
        vm((4, 2, COLS, TOKENS), BF16),
        vm((COLS, TOKENS), BF16),
        vm((COLS, TOKENS), BF16),
        vm((4, 2, COLS, FEATS), BF16),
        vm((COLS, FEATS), BF16),
        vm((COLS, FEATS), BF16),
        vm((2, COLS, FEATS), BF16),
        vm((2, COLS, FEATS), BF16),
        vm((COLS, FEATS), BF16),
        vm((2, COLS, FEATS), F32),
        vm((4, 2, TOKENS, HEAD_DIM), F32),
        vm((4, 4, 2, TOKENS, HEAD_DIM), BF16),
        vm((2, 2, TOKENS, HEAD_DIM), BF16),
        vm((2, 2, TOKENS, HEAD_DIM), BF16),
        vm((4, 2, TOKENS, HEAD_DIM), BF16),
        vm((4, 2, TOKENS, HEAD_DIM), BF16),
        vm((2, 2, TOKENS, HEAD_DIM), BF16),
        vm((2, 2, TOKENS, HEAD_DIM), F32),
        vm((2, TOKENS, HEAD_DIM), F32),
        vm((2, HEAD_DIM, TOKENS), F32),
        vm((2, TOKENS, HEAD_DIM), F32),
        vm((TOKENS, HEAD_DIM), F32),
        pltpu.SemaphoreType.DMA((SEMS,)),
        pltpu.SemaphoreType.DMA((SEMS,)),
    ]
    whole = pl.BlockSpec(memory_space=pltpu.VMEM)
    shape = jax.ShapeDtypeStruct
    return pl.pallas_call(
        kernel,
        name="attention_core",
        out_shape=(
            shape((COLS, TOKENS), F32),
            shape((TOKENS, FEATS), F32),
            shape((TOKENS, FEATS), F32),
            shape((TOKENS, FEATS), F32),
            shape((COLS, FEATS), F32),
        ),
        in_specs=[whole] * 6,
        out_specs=(whole,) * 5,
        scratch_shapes=scratch,
        compiler_params=pltpu.CompilerParams(
            collective_id=0, has_side_effects=True, vmem_limit_bytes=48 << 20
        ),
    )(q, k, v, res, w, ct)


def shards(query_states, key_states, value_states, positions, out_weight, cotangent):
    blocks = lax.axis_size("seq")
    residue = jnp.broadcast_to((positions[0] % blocks).astype(BF16), (16, HEAD_DIM))
    out_t, grad_queries, grad_keys, grad_values, gw_t = fused(
        query_states, key_states, value_states, residue, out_weight.T, cotangent.T
    )
    return out_t.T, grad_queries, grad_keys, grad_values, gw_t.T


def solution(mesh):
    in_specs = (
        P("seq", "fsdp"),
        P("seq", "fsdp"),
        P("seq", "fsdp"),
        P("seq"),
        P("fsdp", "seq"),
        P("seq", "fsdp"),
    )
    out_specs = (
        P("seq", "fsdp"),
        P("seq", "fsdp"),
        P("seq", "fsdp"),
        P("seq", "fsdp"),
        P("fsdp", "seq"),
    )
    return jax.shard_map(shards, mesh=mesh, in_specs=in_specs, out_specs=out_specs, check_vma=False)
```

```python
import math

import jax
import jax.numpy as jnp
from jax import lax
from jax.experimental import pallas as pl
from jax.experimental.pallas import tpu as pltpu
from jax.sharding import PartitionSpec as P

HEAD_DIM = 128
TOKENS = 256
HALF = 128
COLS = 320
FEATS = 256
MESH = pl.DeviceIdType.MESH
BF16 = jnp.bfloat16
F32 = jnp.float32
SCALE = HEAD_DIM ** (-0.5)
SCALE_LOG2 = SCALE * math.log2(math.e)
BLOCKED = -1e30
SEMS = 100


def mm(a, b):
    return jnp.dot(a, b, preferred_element_type=F32)


def mm_nt(a, b):
    return lax.dot_general(a, b, (((1,), (1,)), ((), ())), preferred_element_type=F32)


def mm_tn(a, b):
    return lax.dot_general(a, b, (((0,), (0,)), ((), ())), preferred_element_type=F32)


def kernel(
    pos_ref, q_ref, k_ref, v_ref, w_ref, ct_ref,
    out_hbm, dq_hbm, dk_hbm, dv_hbm, gw_hbm,
    out_ref, dq_ref, dk_ref, dv_ref, gw_ref,
    kvr, res, qt, wt, cot,
    m_ref, l_ref, acc, att_t, att, att_full,
    pga, pga_in, grad_t, grad, delta,
    out_send, out_in, out_fin, out_pair_ici, out_pair_core,
    gw_xsend, gw_xin, gw_send, gw_rin2, gw_lin2, gw_rin, gw_lin,
    df, d_send, d_rin2, d_lin2, d_rin, d_lin, d_x, fin, fin_in,
    dq_t, dq_b, dq_in,
    ss, rs, ls,
):
    seq = lax.axis_index("seq")
    fsdp = lax.axis_index("fsdp")
    xh, y, c = seq // 8, (seq // 2) % 4, seq % 2
    z, xl = fsdp // 2, fsdp % 2
    p = 1 - c
    same = c == xl

    def dev(xh_, y_, c_, z_, xl_):
        return (xh_ * 8 + y_ * 2 + c_, z_ * 2 + xl_)

    yr, yl, y2 = (y + 1) % 4, (y + 3) % 4, (y + 2) % 4
    zr, zl = (z + 1) % 8, (z + 7) % 8
    core_peer = dev(xh, y, p, z, xl)
    xh_peer = dev(1 - xh, y, c, z, xl)
    y_right, y_left = dev(xh, yr, c, z, xl), dev(xh, yl, c, z, xl)
    z_right, z_left = dev(xh, y, c, zr, xl), dev(xh, y, c, zl, xl)
    xl_peers = [dev(xh, y, h, z, 1 - xl) for h in range(2)]
    xl_owner = dev(xh, y, xl, z, 1 - xl)

    used = [0]
    sent = []

    def take(count=1):
        first = used[0]
        used[0] += count
        return first

    def copy(src, dst, to):
        i = take()
        d = pltpu.make_async_remote_copy(
            src_ref=src, dst_ref=dst, send_sem=ss.at[i], recv_sem=rs.at[i],
            device_id=to, device_id_type=MESH,
        )
        d.start()
        sent.append(d)
        return d

    stores = []

    def store(i, src, dst):
        d = pltpu.make_async_copy(src, dst, ls.at[5 + i])
        d.start()
        stores.append(d)

    def arrived(*copies):
        for d in copies:
            d.wait_recv()

    own = y * 4 + xh * 2
    w_own = y * 2 + xh
    mine = pl.ds(pl.multiple_of(c * HEAD_DIM, HEAD_DIM), HEAD_DIM)
    other = pl.ds(pl.multiple_of(p * HEAD_DIM, HEAD_DIM), HEAD_DIM)
    key_rows, value_rows, res_rows = pl.ds(0, TOKENS), pl.ds(TOKENS, TOKENS), pl.ds(2 * TOKENS, 16)
    key_copy = pltpu.make_async_copy(k_ref.at[:, mine], kvr.at[own + c, key_rows], ls.at[0])
    value_copy = pltpu.make_async_copy(v_ref.at[:, mine], kvr.at[own + c, value_rows], ls.at[1])
    query_copy = pltpu.make_async_copy(q_ref.at[:, mine], qt.at[c], ls.at[2])
    weight_copy = pltpu.make_async_copy(w_ref, wt.at[w_own], ls.at[3])
    cot_copy = pltpu.make_async_copy(ct_ref, cot.at[z, c], ls.at[4])
    key_copy.start()
    value_copy.start()

    @pl.when(same)
    def _():
        cot_copy.start()

    query_copy.start()
    weight_copy.start()

    barrier = pltpu.get_barrier_semaphore()
    peers = [core_peer, xh_peer, y_right, y_left, z_right, z_left] + xl_peers
    for peer in peers:
        pl.semaphore_signal(barrier, inc=1, device_id=peer, device_id_type=MESH)
    residue = jnp.full((16, HEAD_DIM), (pos_ref[0] % 16).astype(F32)).astype(BF16)
    res[...] = residue
    kvr[own + c, res_rows, :] = residue
    pl.semaphore_wait(barrier, len(peers))

    core_first = (
        copy(k_ref.at[:, other], kvr.at[own + c, key_rows], core_peer),
        copy(v_ref.at[:, other], kvr.at[own + c, value_rows], core_peer),
        copy(res, kvr.at[own + c, res_rows], core_peer),
    )

    sem_ici, sem_core = take(2), take()
    cot_ici = pltpu.make_async_remote_copy(
        src_ref=ct_ref, dst_ref=cot.at[z, c], send_sem=ss.at[sem_ici], recv_sem=rs.at[sem_ici + c],
        device_id=xl_owner, device_id_type=MESH,
    )
    cot_ici.start()
    sent.append(cot_ici)
    cot_core = pltpu.make_async_remote_copy(
        src_ref=ct_ref, dst_ref=cot.at[z, c], send_sem=ss.at[sem_core], recv_sem=rs.at[sem_core],
        device_id=core_peer, device_id_type=MESH,
    )

    @pl.when(jnp.logical_not(same))
    def _():
        cot_core.start()

    q_core = copy(q_ref.at[:, other], qt.at[c], core_peer)

    def kv_direct(x):
        low, high = kvr.at[y * 4 + x * 2], kvr.at[y * 4 + x * 2 + 1]
        return (
            copy(low, low, y_right), copy(high, high, y_left),
            copy(high, high, y_right), copy(low, low, y_left),
        )

    def kv_forward(x):
        low, high = kvr.at[yl * 4 + x * 2], kvr.at[yr * 4 + x * 2 + 1]
        return copy(low, low, y_right), copy(high, high, y_left)

    def z_pair(right_slot, left_slot, h):
        a, b = cot.at[right_slot, h], cot.at[left_slot, h]
        return copy(a, a, z_right), copy(b, b, z_left)

    key_copy.wait()
    value_copy.wait()
    arrived(*core_first)
    kv_xh = copy(kvr.at[pl.ds(own, 2)], kvr.at[pl.ds(own, 2)], xh_peer)
    kv_mine = kv_direct(xh)
    w_right = copy(w_ref, wt.at[w_own], y_right)
    w_left = copy(w_ref, wt.at[w_own], y_left)

    @pl.when(same)
    def _():
        cot_copy.wait()
        cot_core.wait_recv()

    @pl.when(jnp.logical_not(same))
    def _():
        for h in range(2):
            pltpu.make_async_remote_copy(
                src_ref=ct_ref, dst_ref=cot.at[z, h], send_sem=ss.at[sem_ici],
                recv_sem=rs.at[sem_ici + h], device_id=xl_owner, device_id_type=MESH,
            ).wait_recv()

    z_one = [z_pair(z, z, h) for h in range(2)]
    w_xh = [copy(w_ref, wt.at[w_own], xh_peer)]

    acc[...] = jnp.zeros_like(acc)
    l_ref[...] = jnp.zeros_like(l_ref)
    m_ref[...] = jnp.full_like(m_ref, BLOCKED)
    pga[...] = jnp.zeros_like(pga)
    dq_t[...] = jnp.zeros_like(dq_t)
    query_copy.wait()
    weight_copy.wait()
    arrived(q_core)

    arrived(*kv_mine[:2])
    kv_mine_far = kv_forward(xh)
    arrived(kv_xh)
    kv_other = kv_direct(1 - xh)
    arrived(*z_one[0])
    z_two = [z_pair(zl, zr, 0)]

    ahead = (
        lax.broadcasted_iota(jnp.int32, (1, HALF, TOKENS), 2) % HALF
        - lax.broadcasted_iota(jnp.int32, (1, HALF, TOKENS), 1)
    )

    def residue_rows(slot, count):
        return kvr[pl.ds(slot, count), pl.ds(2 * TOKENS, 16), :].astype(F32)[:, 0:1, :]

    query_res = residue_rows(own, 2)
    query_res = jnp.concatenate([query_res[0:1], query_res[1:2]], axis=2)

    def tile_scores(yy, qi, ki):
        key_res = residue_rows(yy * 4, 4)
        key_res = jnp.concatenate([key_res, key_res], axis=2)
        bound = jnp.where(key_res <= query_res, 0, 1) - jnp.where(qi > ki, 4 * HALF, 0)
        rows = pl.multiple_of(ki * HALF, HALF)
        keys = kvr[pl.ds(yy * 4, 4), pl.ds(rows, HALF), :].reshape(4 * HALF, HEAD_DIM)
        values = kvr[pl.ds(yy * 4, 4), pl.ds(TOKENS + rows, HALF), :].reshape(4 * HALF, HEAD_DIM)
        query_rows = pl.ds(pl.multiple_of(qi * HALF, HALF), HALF)
        queries = qt[:, query_rows, :].reshape(TOKENS, HEAD_DIM)
        scores = mm_nt(keys, queries) * SCALE_LOG2
        seen = ahead >= bound
        scores = jnp.where(seen, scores.reshape(4, HALF, TOKENS), BLOCKED)
        return scores.reshape(4 * HALF, TOKENS), keys, values, queries

    def forward(yy):
        def tile(t, carry):
            qi, ki = (t + 1) // 2, t // 2
            scores, _, values, _ = tile_scores(yy, qi, ki)
            old = m_ref[qi]
            new = jnp.maximum(old, jnp.max(scores, axis=0, keepdims=True))
            probs = jnp.exp2(scores - new)
            shrink = jnp.exp2(old - new)
            m_ref[qi] = new
            l_ref[qi] = l_ref[qi] * shrink + jnp.sum(probs, axis=0, keepdims=True)
            acc[qi] = acc[qi] * shrink + mm_tn(values, probs.astype(BF16))
            return carry

        lax.fori_loop(0, 3, tile, 0)

    forward(y)
    arrived(w_right, w_left)
    w_low, w_high = wt.at[yl * 2 + xh, pl.ds(0, 160)], wt.at[yr * 2 + xh, pl.ds(160, 160)]
    w_far = (copy(w_low, w_low, y_right), copy(w_high, w_high, y_left))
    w_xh.append(copy(wt.at[yl * 2 + xh], wt.at[yl * 2 + xh], xh_peer))
    w_xh.append(copy(wt.at[yr * 2 + xh], wt.at[yr * 2 + xh], xh_peer))
    arrived(*z_one[1])
    z_two.append(z_pair(zl, zr, 1))
    arrived(*z_two[0])
    z_three = [z_pair((z + 6) % 8, (z + 2) % 8, 0)]
    arrived(*kv_other[:2])
    kv_other_far = kv_forward(1 - xh)
    arrived(*kv_mine[2:], *kv_other[2:])
    forward(yl)
    arrived(*w_far)
    w_xh.append(copy(wt.at[y2 * 2 + xh], wt.at[y2 * 2 + xh], xh_peer))
    arrived(*z_two[1])
    z_three.append(z_pair((z + 6) % 8, (z + 2) % 8, 1))
    forward(yr)
    arrived(*z_three[0])
    z_four = [copy(cot.at[(z + 5) % 8, 0], cot.at[(z + 5) % 8, 0], z_right)]
    arrived(*kv_mine_far, *kv_other_far)
    forward(y2)
    arrived(*z_three[1])
    z_four.append(copy(cot.at[(z + 3) % 8, 1], cot.at[(z + 3) % 8, 1], z_left))

    for qi in range(2):
        total = l_ref[qi]
        rows = (acc[qi] / total).astype(BF16)
        att_t[qi] = rows
        m_ref[qi] = m_ref[qi] + jnp.log2(total)
        wide = rows.astype(F32)
        for h in range(2):
            att[c, h, pl.ds(qi * HALF, HALF), :] = wide[:, h * HALF:(h + 1) * HALF].T.astype(BF16)
    att_core = copy(att.at[c], att.at[c], core_peer)
    arrived(*w_xh)
    arrived(att_core)
    for h in range(2):
        att_full[h] = jnp.concatenate([att[0, h], att[1, h]], axis=1)

    def w_block(i):
        return wt[(i % 4) * 2 + i // 4]

    def out_term(i, h):
        return mm_nt(w_block(i), att_full[h])

    def out_hop(step, long_chain, got):
        sends = []
        for side in range(2):
            h = side if long_chain else 1 - side
            target = (z + 4 - step) % 8 if side == 0 else (z + 4 + step) % 8
            term = out_term(target, h)
            if got is not None:
                arrived(got[side])
                term = term + out_in[side, step - 1, h].astype(F32)
            out_send[side, step, h] = term.astype(BF16)
            sends.append(
                copy(out_send.at[side, step, h], out_in.at[side, step, h], z_left if side else z_right)
            )
        return sends

    long_0 = out_hop(0, True, None)
    short_1 = out_hop(1, False, None)
    arrived(*z_four)

    def width_step(i, carry):
        weight = w_block(i)
        for h in range(2):
            term = mm_tn(weight, cot[i, h])
            pga[0, h] += term[:HEAD_DIM]
            pga[1, h] += term[HEAD_DIM:]
        return carry

    lax.fori_loop(0, 8, width_step, 0)
    pga_core = copy(pga.at[p], pga_in, core_peer)

    def gw_term(x, yy):
        i = x * 4 + yy
        return mm(cot[i, 0], att_full[0]) + mm(cot[i, 1], att_full[1])

    gw_over = []
    for i, yy in enumerate((y2, yr, yl, y)):
        gw_xsend[i] = gw_term(1 - xh, yy).astype(BF16)
        gw_over.append(copy(gw_xsend.at[i], gw_xin.at[i], xh_peer))
    long_1 = out_hop(1, True, long_0)

    arrived(pga_core)
    for h in range(2):
        rows = (pga[c, h] + pga_in[h]).astype(BF16)
        for qi in range(2):
            grad_t[qi, :, h * HALF:(h + 1) * HALF] = rows[:, qi * HALF:(qi + 1) * HALF]
    for qi in range(2):
        wide = grad_t[qi].astype(F32)
        delta[qi] = jnp.sum(wide * att_t[qi].astype(F32), axis=0, keepdims=True)
        grad[qi] = wide.T.astype(BF16)

    def backward(yy):
        df[...] = jnp.zeros_like(df)

        def tile(t, carry):
            qi, ki = (t + 1) // 2, t // 2
            scores, keys, values, queries = tile_scores(yy, qi, ki)
            probs = jnp.exp2(scores - m_ref[qi])
            grad_probs = mm(values, grad_t[qi])
            grad_scores = (probs * (grad_probs - delta[qi])).astype(BF16)
            rows = pl.ds(pl.multiple_of(ki * HALF, HALF), HALF)
            grad_keys = mm(grad_scores, queries).reshape(4, HALF, HEAD_DIM)
            grad_values = mm(probs.astype(BF16), grad[qi]).reshape(4, HALF, HEAD_DIM)
            df[:, 0, rows, :] += grad_keys
            df[:, 1, rows, :] += grad_values
            dq_t[qi] += mm_tn(keys, grad_scores)
            return carry

        lax.fori_loop(0, 3, tile, 0)

    near = pl.ds(2 * xh, 2)
    over = pl.ds(2 * (1 - xh), 2)

    backward(y2)
    d_send[0, 0] = df[near].astype(BF16)
    d_far_right = copy(d_send.at[0, 0], d_rin2, y_right)
    d_send[0, 1] = df[over].astype(BF16)
    d_far_left = copy(d_send.at[0, 1], d_lin2, y_left)
    short_2 = out_hop(2, False, short_1)

    arrived(gw_over[0])
    gw_send[0] = (gw_term(xh, y2) + gw_xin[0].astype(F32)).astype(BF16)
    gw_far = (
        copy(gw_send.at[0, pl.ds(0, 160)], gw_rin2, y_right),
        copy(gw_send.at[0, pl.ds(160, 160)], gw_lin2, y_left),
    )

    backward(yr)
    d_send[1, 1] = df[over].astype(BF16)
    d_right = [copy(d_send.at[1, 1], d_rin.at[1], y_right)]
    long_2 = out_hop(2, True, long_1)
    arrived(d_far_right)
    d_send[1, 0] = (df[near] + d_rin2[...].astype(F32)).astype(BF16)
    d_right.append(copy(d_send.at[1, 0], d_rin.at[0], y_right))

    backward(yl)
    arrived(d_far_left)
    d_send[2, 1] = (df[over] + d_lin2[...].astype(F32)).astype(BF16)
    d_left = [copy(d_send.at[2, 1], d_lin.at[1], y_left)]
    d_send[2, 0] = df[near].astype(BF16)
    d_left.append(copy(d_send.at[2, 0], d_lin.at[0], y_left))
    short_3 = out_hop(3, False, short_2)

    arrived(*gw_far)
    arrived(*gw_over[1:])
    low, high = pl.ds(0, 160), pl.ds(160, 160)
    term = gw_term(xh, yr) + gw_xin[1].astype(F32)
    gw_send[1, low] = (term[:160] + gw_rin2[...].astype(F32)).astype(BF16)
    gw_send[1, high] = term[160:].astype(BF16)
    term = gw_term(xh, yl) + gw_xin[2].astype(F32)
    gw_send[2, low] = term[:160].astype(BF16)
    gw_send[2, high] = (term[160:] + gw_lin2[...].astype(F32)).astype(BF16)
    gw_near = (copy(gw_send.at[1], gw_rin, y_right), copy(gw_send.at[2], gw_lin, y_left))

    backward(y)
    long_3 = out_hop(3, True, long_2)
    for qi in range(2):
        for h in range(2):
            dq_b[h, pl.ds(qi * HALF, HALF), :] = dq_t[qi, :, h * HALF:(h + 1) * HALF].T * SCALE
    dq_core = copy(dq_b.at[p], dq_in, core_peer)

    arrived(d_right[0], d_left[0])
    d_send[3, 1] = (df[over] + d_rin[1].astype(F32) + d_lin[1].astype(F32)).astype(BF16)
    d_over = copy(d_send.at[3, 1], d_x, xh_peer)

    first = c == 0

    def place(ref, mine, theirs):
        ref[:, :HEAD_DIM] = jnp.where(first, mine, theirs)
        ref[:, HEAD_DIM:] = jnp.where(first, theirs, mine)

    arrived(dq_core)
    place(dq_ref, dq_b[c], dq_in[...])
    store(1, dq_ref, dq_hbm)

    arrived(*short_3)
    for h in range(2):
        out_fin[h] = out_term(z, h) + out_in[1 - h, 3, h].astype(F32)
    arrived(*long_3)
    for h in range(2):
        out_send[0, 4, h] = (out_fin[h] + out_in[h, 3, h].astype(F32)).astype(BF16)
    pair_ici, pair_core = take(2), take()
    to_peers = [
        pltpu.make_async_remote_copy(
            src_ref=out_send.at[0, 4, h], dst_ref=out_pair_ici, send_sem=ss.at[pair_ici + h],
            recv_sem=rs.at[pair_ici], device_id=xl_peers[h], device_id_type=MESH,
        )
        for h in range(2)
    ]
    to_core = pltpu.make_async_remote_copy(
        src_ref=out_send.at[0, 4, p], dst_ref=out_pair_core, send_sem=ss.at[pair_core],
        recv_sem=rs.at[pair_core], device_id=core_peer, device_id_type=MESH,
    )

    @pl.when(same)
    def _():
        to_core.start()

    @pl.when(jnp.logical_not(same))
    def _():
        to_peers[0].start()
        to_peers[1].start()

    arrived(d_right[1], d_left[1])
    arrived(d_over)
    for part in range(2):
        total = (
            df[near, part]
            + d_rin[0, :, part].astype(F32)
            + d_lin[0, :, part].astype(F32)
            + d_x[:, part].astype(F32)
        )
        fin[:, part] = total * SCALE if part == 0 else total
    fin_core = copy(fin.at[p], fin_in, core_peer)

    arrived(*gw_near)
    gw_ref[...] = (
        gw_term(xh, y) + gw_xin[3].astype(F32) + gw_rin[...].astype(F32) + gw_lin[...].astype(F32)
    )
    store(4, gw_ref, gw_hbm)

    arrived(fin_core)
    place(dk_ref, fin[c, 0], fin_in[0])
    store(2, dk_ref, dk_hbm)
    place(dv_ref, fin[c, 1], fin_in[1])
    store(3, dv_ref, dv_hbm)

    arrived(to_peers[0])

    @pl.when(same)
    def _():
        out_ref[...] = out_send[0, 4, c].astype(F32) + out_pair_ici[...].astype(F32)
        to_core.wait_send()

    @pl.when(jnp.logical_not(same))
    def _():
        to_core.wait_recv()
        out_ref[...] = out_pair_core[...].astype(F32) + out_pair_ici[...].astype(F32)
        to_peers[0].wait_send()
        to_peers[1].wait_send()
        cot_core.wait_send()

    store(0, out_ref, out_hbm)
    for d in sent:
        d.wait_send()
    for d in stores:
        d.wait()
    assert used[0] <= SEMS, used[0]


def fused(pos, q, k, v, w, ct):
    vm = pltpu.VMEM
    scratch = [
        vm((16, 2 * TOKENS + 16, HEAD_DIM), BF16),
        vm((16, HEAD_DIM), BF16),
        vm((2, TOKENS, HEAD_DIM), BF16),
        vm((8, COLS, FEATS), BF16),
        vm((8, 2, COLS, TOKENS), BF16),
        vm((2, 1, TOKENS), F32),
        vm((2, 1, TOKENS), F32),
        vm((2, HEAD_DIM, TOKENS), F32),
        vm((2, HEAD_DIM, TOKENS), BF16),
        vm((2, 2, TOKENS, HEAD_DIM), BF16),
        vm((2, TOKENS, FEATS), BF16),
        vm((2, 2, HEAD_DIM, TOKENS), F32),
        vm((2, HEAD_DIM, TOKENS), F32),
        vm((2, HEAD_DIM, TOKENS), BF16),
        vm((2, TOKENS, HEAD_DIM), BF16),
        vm((2, 1, TOKENS), F32),
        vm((2, 5, 2, COLS, TOKENS), BF16),
        vm((2, 4, 2, COLS, TOKENS), BF16),
        vm((2, COLS, TOKENS), F32),
        vm((COLS, TOKENS), BF16),
        vm((COLS, TOKENS), BF16),
        vm((4, COLS, FEATS), BF16),
        vm((4, COLS, FEATS), BF16),
        vm((3, COLS, FEATS), BF16),
        vm((COLS // 2, FEATS), BF16),
        vm((COLS // 2, FEATS), BF16),
        vm((COLS, FEATS), BF16),
        vm((COLS, FEATS), BF16),
        vm((4, 2, TOKENS, HEAD_DIM), F32),
        vm((4, 2, 2, 2, TOKENS, HEAD_DIM), BF16),
        vm((2, 2, TOKENS, HEAD_DIM), BF16),
        vm((2, 2, TOKENS, HEAD_DIM), BF16),
        vm((2, 2, 2, TOKENS, HEAD_DIM), BF16),
        vm((2, 2, 2, TOKENS, HEAD_DIM), BF16),
        vm((2, 2, TOKENS, HEAD_DIM), BF16),
        vm((2, 2, TOKENS, HEAD_DIM), F32),
        vm((2, TOKENS, HEAD_DIM), F32),
        vm((2, HEAD_DIM, TOKENS), F32),
        vm((2, TOKENS, HEAD_DIM), F32),
        vm((TOKENS, HEAD_DIM), F32),
        pltpu.SemaphoreType.DMA((SEMS,)),
        pltpu.SemaphoreType.DMA((SEMS,)),
        pltpu.SemaphoreType.DMA((10,)),
    ]
    in_hbm = pl.BlockSpec(memory_space=pl.ANY)
    return pl.pallas_call(
        kernel,
        name="attention_core",
        out_shape=OUT_SHAPES,
        in_specs=[pl.BlockSpec(memory_space=pltpu.SMEM)] + [in_hbm] * 5,
        out_specs=(in_hbm,) * 5,
        scratch_shapes=[vm(d.shape, d.dtype) for d in OUT_SHAPES] + scratch,
        compiler_params=pltpu.CompilerParams(
            collective_id=0, has_side_effects=True, vmem_limit_bytes=62 << 20
        ),
    )(pos, q, k, v, w, ct)


OUT_SHAPES = (
    jax.ShapeDtypeStruct((COLS, TOKENS), F32),
    jax.ShapeDtypeStruct((TOKENS, FEATS), F32),
    jax.ShapeDtypeStruct((TOKENS, FEATS), F32),
    jax.ShapeDtypeStruct((TOKENS, FEATS), F32),
    jax.ShapeDtypeStruct((COLS, FEATS), F32),
)


def store_kernel(*refs):
    results, outs, held, sems = refs[:5], refs[5:10], refs[10:15], refs[15]
    loads = [pltpu.make_async_copy(results[i], held[i], sems.at[0, i]) for i in range(5)]
    stores = [pltpu.make_async_copy(held[i], outs[i], sems.at[1, i]) for i in range(5)]
    for d in loads:
        d.start()
    for load, store in zip(loads, stores):
        load.wait()
        store.start()
    for d in stores:
        d.wait()


def stored(*results):
    return pl.pallas_call(
        store_kernel,
        name="store_results",
        out_shape=OUT_SHAPES,
        in_specs=[pl.BlockSpec(memory_space=pl.ANY)] * 5,
        out_specs=(pl.BlockSpec(memory_space=pl.ANY),) * 5,
        scratch_shapes=[pltpu.VMEM(d.shape, d.dtype) for d in OUT_SHAPES]
        + [pltpu.SemaphoreType.DMA((2, 5))],
        compiler_params=pltpu.CompilerParams(vmem_limit_bytes=62 << 20),
    )(*results)


def shards(query_states, key_states, value_states, positions, out_weight, cotangent):
    results = fused(
        positions, query_states, key_states, value_states, out_weight.T, cotangent.T
    )
    out_t, grad_queries, grad_keys, grad_values, gw_t = stored(*results)
    return out_t.T, grad_queries, grad_keys, grad_values, gw_t.T


def solution(mesh):
    in_specs = (
        P("seq", "fsdp"),
        P("seq", "fsdp"),
        P("seq", "fsdp"),
        P("seq"),
        P("fsdp", "seq"),
        P("seq", "fsdp"),
    )
    out_specs = (
        P("seq", "fsdp"),
        P("seq", "fsdp"),
        P("seq", "fsdp"),
        P("seq", "fsdp"),
        P("fsdp", "seq"),
    )
    return jax.shard_map(shards, mesh=mesh, in_specs=in_specs, out_specs=out_specs, check_vma=False)
```

```python
import math

import jax
import jax.numpy as jnp
from jax import lax
from jax.experimental import pallas as pl
from jax.experimental.pallas import tpu as pltpu
from jax.sharding import PartitionSpec as P

HEAD_DIM = 128
TOKENS = 256
HALF = 128
COLS = 320
FEATS = 256
MESH = pl.DeviceIdType.MESH
BF16 = jnp.bfloat16
F32 = jnp.float32
SCALE = HEAD_DIM ** (-0.5)
SCALE_LOG2 = SCALE * math.log2(math.e)
BLOCKED = -1e30
SEMS = 112


def mm(a, b):
    return jnp.dot(a, b, preferred_element_type=F32)


def mm_nt(a, b):
    return lax.dot_general(a, b, (((1,), (1,)), ((), ())), preferred_element_type=F32)


def mm_tn(a, b):
    return lax.dot_general(a, b, (((0,), (0,)), ((), ())), preferred_element_type=F32)


def kernel(
    pos_ref, q_ref, k_ref, v_ref, w_ref, ct_ref,
    out_hbm, dq_hbm, dk_hbm, dv_hbm, gw_hbm,
    out_ref, dq_ref, dk_ref, dv_ref, gw_ref,
    kvr, res, qt, wt, cot,
    m_ref, l_ref, acc, att_t, att, att_full,
    pga, pga_in, grad_t, grad, delta,
    out_send, out_in, out_fin, out_pair_ici, out_pair_core,
    gw_xsend, gw_xin, gw_send, gw_rin2, gw_lin2, gw_rin, gw_lin,
    df, df_right, d_send, d_rin2, d_lin2, d_rin, d_lin, d_x, fin, fin_in,
    dq_t, dq_b, dq_in,
    ss, rs, ls,
):
    seq = lax.axis_index("seq")
    fsdp = lax.axis_index("fsdp")
    xh, y, c = seq // 8, (seq // 2) % 4, seq % 2
    z, xl = fsdp // 2, fsdp % 2
    p = 1 - c
    same = c == xl

    def dev(xh_, y_, c_, z_, xl_):
        return (xh_ * 8 + y_ * 2 + c_, z_ * 2 + xl_)

    yr, yl, y2 = (y + 1) % 4, (y + 3) % 4, (y + 2) % 4
    zr, zl = (z + 1) % 8, (z + 7) % 8
    core_peer = dev(xh, y, p, z, xl)
    xh_peer = dev(1 - xh, y, c, z, xl)
    y_right, y_left = dev(xh, yr, c, z, xl), dev(xh, yl, c, z, xl)
    z_right, z_left = dev(xh, y, c, zr, xl), dev(xh, y, c, zl, xl)
    xl_peers = [dev(xh, y, h, z, 1 - xl) for h in range(2)]
    xl_owner = dev(xh, y, xl, z, 1 - xl)

    used = [0]
    sent = []

    def take(count=1):
        first = used[0]
        used[0] += count
        return first

    def copy(src, dst, to):
        i = take()
        d = pltpu.make_async_remote_copy(
            src_ref=src, dst_ref=dst, send_sem=ss.at[i], recv_sem=rs.at[i],
            device_id=to, device_id_type=MESH,
        )
        d.start()
        sent.append(d)
        return d

    stores = []

    def store(i, src, dst):
        d = pltpu.make_async_copy(src, dst, ls.at[5 + i])
        d.start()
        stores.append(d)

    def arrived(*copies):
        for d in copies:
            d.wait_recv()

    own = y * 4 + xh * 2
    w_own = y * 2 + xh
    mine = pl.ds(pl.multiple_of(c * HEAD_DIM, HEAD_DIM), HEAD_DIM)
    other = pl.ds(pl.multiple_of(p * HEAD_DIM, HEAD_DIM), HEAD_DIM)
    key_rows, value_rows, res_rows = pl.ds(0, TOKENS), pl.ds(TOKENS, TOKENS), pl.ds(2 * TOKENS, 16)
    key_copy = pltpu.make_async_copy(k_ref.at[:, mine], kvr.at[own + c, key_rows], ls.at[0])
    value_copy = pltpu.make_async_copy(v_ref.at[:, mine], kvr.at[own + c, value_rows], ls.at[1])
    query_copy = pltpu.make_async_copy(q_ref.at[:, mine], qt.at[c], ls.at[2])
    weight_copy = pltpu.make_async_copy(w_ref, wt.at[w_own], ls.at[3])
    cot_copy = pltpu.make_async_copy(ct_ref, cot.at[z, c], ls.at[4])
    key_copy.start()
    value_copy.start()

    @pl.when(same)
    def _():
        cot_copy.start()

    query_copy.start()
    weight_copy.start()

    barrier = pltpu.get_barrier_semaphore()
    z_cross = [dev(xh, y, p, zr, xl), dev(xh, y, p, zl, xl)]
    peers = [core_peer, xh_peer, y_right, y_left, z_right, z_left] + xl_peers + z_cross
    for peer in peers:
        pl.semaphore_signal(barrier, inc=1, device_id=peer, device_id_type=MESH)
    residue = jnp.full((16, HEAD_DIM), (pos_ref[0] % 16).astype(F32)).astype(BF16)
    res[...] = residue
    kvr[own + c, res_rows, :] = residue
    key_copy.wait()
    value_copy.wait()
    pl.semaphore_wait(barrier, len(peers))

    sem_ici, sem_core, sem_z = take(2), take(), take(4)
    z_owner = [dev(xh, y, xl, zr, xl), dev(xh, y, xl, zl, xl)]

    def cot_copy_to(h, src, to, send, recv):
        return pltpu.make_async_remote_copy(
            src_ref=src, dst_ref=cot.at[z, h], send_sem=ss.at[send], recv_sem=rs.at[recv],
            device_id=to, device_id_type=MESH,
        )

    cot_ici = cot_copy_to(c, ct_ref, xl_owner, sem_ici, sem_ici + c)
    cot_core = cot_copy_to(c, ct_ref, core_peer, sem_core, sem_core)
    cot_z = [
        cot_copy_to(c, ct_ref, z_owner[side], sem_z + side, sem_z + 2 * side + c) for side in range(2)
    ]
    sem_own = take(4)
    cot_own = [
        [
            cot_copy_to(h, cot.at[z, h], to, sem_own + 2 * side + h, sem_z + 2 * side + h)
            for side, to in enumerate((z_right, z_left))
        ]
        for h in range(2)
    ]
    cot_ici.start()

    core_first = (
        copy(k_ref.at[:, other], kvr.at[own + c, key_rows], core_peer),
        copy(v_ref.at[:, other], kvr.at[own + c, value_rows], core_peer),
        copy(res, kvr.at[own + c, res_rows], core_peer),
    )

    def kv_send(slot, *targets):
        block = kvr.at[slot]
        return [copy(block, block, to) for to in targets]

    kv_c = kv_send(own + c, y_right, y_left, xh_peer)
    for d in cot_z:
        d.start()

    @pl.when(jnp.logical_not(same))
    def _():
        cot_core.start()

    w_right = copy(w_ref, wt.at[w_own], y_right)
    w_left = copy(w_ref, wt.at[w_own], y_left)
    q_core = copy(q_ref.at[:, other], qt.at[c], core_peer)

    def z_pair(right_slot, left_slot, h):
        a, b = cot.at[right_slot, h], cot.at[left_slot, h]
        return copy(a, a, z_right), copy(b, b, z_left)

    arrived(*core_first)
    kv_p = kv_send(own + p, y_right, y_left, xh_peer)

    @pl.when(same)
    def _():
        cot_copy.wait()
        cot_core.wait_recv()

    @pl.when(jnp.logical_not(same))
    def _():
        for h in range(2):
            cot_copy_to(h, ct_ref, xl_owner, sem_ici, sem_ici + h).wait_recv()
            for d in cot_own[h]:
                d.start()

    w_xh = [copy(w_ref, wt.at[w_own], xh_peer)]

    acc[...] = jnp.zeros_like(acc)
    l_ref[...] = jnp.zeros_like(l_ref)
    m_ref[...] = jnp.full_like(m_ref, BLOCKED)
    pga[...] = jnp.zeros_like(pga)
    dq_t[...] = jnp.zeros_like(dq_t)
    query_copy.wait()
    weight_copy.wait()
    arrived(q_core)

    kv_far = []
    over_own = y * 4 + (1 - xh) * 2

    arrived(kv_c[0])
    kv_far += kv_send(yl * 4 + xh * 2 + c, y_right)
    arrived(kv_c[1], kv_c[2])
    kv_over_c = kv_send(over_own + c, y_right, y_left)
    z_two = []
    for h in range(2):
        for d in cot_own[h]:
            d.wait_recv()
        z_two.append(z_pair(zl, zr, h))
    arrived(w_right, w_left)
    w_low, w_high = wt.at[yl * 2 + xh, pl.ds(0, 160)], wt.at[yr * 2 + xh, pl.ds(160, 160)]
    w_far = (copy(w_low, w_low, y_right), copy(w_high, w_high, y_left))
    w_xh.append(copy(wt.at[yl * 2 + xh], wt.at[yl * 2 + xh], xh_peer))
    w_xh.append(copy(wt.at[yr * 2 + xh], wt.at[yr * 2 + xh], xh_peer))
    arrived(*kv_p)
    kv_over_p = kv_send(over_own + p, y_right, y_left)
    kv_far += kv_send(yr * 4 + xh * 2 + p, y_left)

    ahead = (
        lax.broadcasted_iota(jnp.int32, (1, HALF, TOKENS), 2) % HALF
        - lax.broadcasted_iota(jnp.int32, (1, HALF, TOKENS), 1)
    )

    def residue_rows(slot, count):
        return kvr[pl.ds(slot, count), pl.ds(2 * TOKENS, 16), :].astype(F32)[:, 0:1, :]

    query_res = residue_rows(own, 2)
    query_res = jnp.concatenate([query_res[0:1], query_res[1:2]], axis=2)

    def tile_scores(yy, qi, ki):
        key_res = residue_rows(yy * 4, 4)
        key_res = jnp.concatenate([key_res, key_res], axis=2)
        bound = jnp.where(key_res <= query_res, 0, 1) - jnp.where(qi > ki, 4 * HALF, 0)
        rows = pl.multiple_of(ki * HALF, HALF)
        keys = kvr[pl.ds(yy * 4, 4), pl.ds(rows, HALF), :].reshape(4 * HALF, HEAD_DIM)
        values = kvr[pl.ds(yy * 4, 4), pl.ds(TOKENS + rows, HALF), :].reshape(4 * HALF, HEAD_DIM)
        query_rows = pl.ds(pl.multiple_of(qi * HALF, HALF), HALF)
        queries = qt[:, query_rows, :].reshape(TOKENS, HEAD_DIM)
        scores = mm_nt(keys, queries) * SCALE_LOG2
        seen = ahead >= bound
        scores = jnp.where(seen, scores.reshape(4, HALF, TOKENS), BLOCKED)
        return scores.reshape(4 * HALF, TOKENS), keys, values, queries

    def forward(yy):
        def tile(t, carry):
            qi, ki = (t + 1) // 2, t // 2
            scores, _, values, _ = tile_scores(yy, qi, ki)
            old = m_ref[qi]
            new = jnp.maximum(old, jnp.max(scores, axis=0, keepdims=True))
            probs = jnp.exp2(scores - new)
            shrink = jnp.exp2(old - new)
            m_ref[qi] = new
            l_ref[qi] = l_ref[qi] * shrink + jnp.sum(probs, axis=0, keepdims=True)
            acc[qi] = acc[qi] * shrink + mm_tn(values, probs.astype(BF16))
            return carry

        lax.fori_loop(0, 3, tile, 0)

    forward(y)
    arrived(*z_two[0])
    z_three = [z_pair((z + 6) % 8, (z + 2) % 8, 0)]
    arrived(*kv_over_c)
    kv_far += kv_send(yl * 4 + (1 - xh) * 2 + c, y_right)
    arrived(*z_two[1])
    z_three.append(z_pair((z + 6) % 8, (z + 2) % 8, 1))
    arrived(*w_far)
    w_xh.append(copy(wt.at[y2 * 2 + xh], wt.at[y2 * 2 + xh], xh_peer))
    arrived(*kv_over_p)
    kv_far += kv_send(yr * 4 + (1 - xh) * 2 + p, y_left)
    forward(yl)
    arrived(*z_three[0])
    z_four = [copy(cot.at[(z + 5) % 8, 0], cot.at[(z + 5) % 8, 0], z_right)]
    forward(yr)
    arrived(*z_three[1])
    z_four.append(copy(cot.at[(z + 3) % 8, 1], cot.at[(z + 3) % 8, 1], z_left))
    arrived(*kv_far)
    forward(y2)

    for qi in range(2):
        total = l_ref[qi]
        rows = (acc[qi] / total).astype(BF16)
        att_t[qi] = rows
        m_ref[qi] = m_ref[qi] + jnp.log2(total)
        wide = rows.astype(F32)
        for h in range(2):
            att[c, h, pl.ds(qi * HALF, HALF), :] = wide[:, h * HALF:(h + 1) * HALF].T.astype(BF16)
    att_core = copy(att.at[c], att.at[c], core_peer)
    arrived(*w_xh)

    def w_block(i):
        return wt[(i % 4) * 2 + i // 4]

    def width_step(k, carry):
        i = (z + 5 + k) % 8
        weight = w_block(i)
        for h in range(2):
            term = mm_tn(weight, cot[i, h])
            pga[0, h] += term[:HEAD_DIM]
            pga[1, h] += term[HEAD_DIM:]
        return carry

    lax.fori_loop(0, 7, width_step, 0)
    arrived(att_core)
    for h in range(2):
        att_full[h] = jnp.concatenate([att[0, h], att[1, h]], axis=1)

    def out_term(i, h):
        return mm_nt(w_block(i), att_full[h])

    def out_hop(step, long_chain, got):
        sends = []
        for side in range(2):
            h = side if long_chain else 1 - side
            target = (z + 4 - step) % 8 if side == 0 else (z + 4 + step) % 8
            term = out_term(target, h)
            if got is not None:
                arrived(got[side])
                term = term + out_in[side, step - 1, h].astype(F32)
            out_send[side, step, h] = term.astype(BF16)
            sends.append(
                copy(out_send.at[side, step, h], out_in.at[side, step, h], z_left if side else z_right)
            )
        return sends

    long_0 = out_hop(0, True, None)
    short_1 = out_hop(1, False, None)
    arrived(*z_four)

    width_step(7, 0)
    pga_core = copy(pga.at[p], pga_in, core_peer)

    def gw_term(x, yy):
        i = x * 4 + yy
        return mm(cot[i, 0], att_full[0]) + mm(cot[i, 1], att_full[1])

    gw_over = []
    for i, yy in enumerate((y2, yr, yl, y)):
        gw_xsend[i] = gw_term(1 - xh, yy).astype(BF16)
        gw_over.append(copy(gw_xsend.at[i], gw_xin.at[i], xh_peer))

    arrived(pga_core)
    for h in range(2):
        rows = (pga[c, h] + pga_in[h]).astype(BF16)
        for qi in range(2):
            grad_t[qi, :, h * HALF:(h + 1) * HALF] = rows[:, qi * HALF:(qi + 1) * HALF]
    for qi in range(2):
        wide = grad_t[qi].astype(F32)
        delta[qi] = jnp.sum(wide * att_t[qi].astype(F32), axis=0, keepdims=True)
        grad[qi] = wide.T.astype(BF16)

    def backward(yy, df):
        df[...] = jnp.zeros_like(df)

        def tile(t, carry):
            qi, ki = (t + 1) // 2, t // 2
            scores, keys, values, queries = tile_scores(yy, qi, ki)
            probs = jnp.exp2(scores - m_ref[qi])
            grad_probs = mm(values, grad_t[qi])
            grad_scores = (probs * (grad_probs - delta[qi])).astype(BF16)
            rows = pl.ds(pl.multiple_of(ki * HALF, HALF), HALF)
            grad_keys = mm(grad_scores, queries).reshape(4, HALF, HEAD_DIM)
            grad_values = mm(probs.astype(BF16), grad[qi]).reshape(4, HALF, HEAD_DIM)
            df[:, 0, rows, :] += grad_keys
            df[:, 1, rows, :] += grad_values
            dq_t[qi] += mm_tn(keys, grad_scores)
            return carry

        lax.fori_loop(0, 3, tile, 0)

    near = pl.ds(2 * xh, 2)
    over = pl.ds(2 * (1 - xh), 2)

    backward(y2, df)
    d_send[0, 0] = df[near].astype(BF16)
    d_far_right = copy(d_send.at[0, 0], d_rin2, y_right)
    d_send[0, 1] = df[over].astype(BF16)
    d_far_left = copy(d_send.at[0, 1], d_lin2, y_left)
    long_1 = out_hop(1, True, long_0)

    arrived(gw_over[0])
    gw_send[0] = (gw_term(xh, y2) + gw_xin[0].astype(F32)).astype(BF16)
    gw_far = (
        copy(gw_send.at[0, pl.ds(0, 160)], gw_rin2, y_right),
        copy(gw_send.at[0, pl.ds(160, 160)], gw_lin2, y_left),
    )

    backward(yr, df_right)
    d_send[1, 1] = df_right[over].astype(BF16)
    d_right = [copy(d_send.at[1, 1], d_rin.at[1], y_right)]
    short_2 = out_hop(2, False, short_1)
    backward(yl, df)
    arrived(d_far_left)
    d_send[2, 1] = (df[over] + d_lin2[...].astype(F32)).astype(BF16)
    d_left = [copy(d_send.at[2, 1], d_lin.at[1], y_left)]
    arrived(d_far_right)
    d_send[1, 0] = (df_right[near] + d_rin2[...].astype(F32)).astype(BF16)
    d_right.append(copy(d_send.at[1, 0], d_rin.at[0], y_right))
    d_send[2, 0] = df[near].astype(BF16)
    d_left.append(copy(d_send.at[2, 0], d_lin.at[0], y_left))
    long_2 = out_hop(2, True, long_1)

    arrived(*gw_far)
    arrived(*gw_over[1:])
    low, high = pl.ds(0, 160), pl.ds(160, 160)
    term = gw_term(xh, yr) + gw_xin[1].astype(F32)
    gw_send[1, low] = (term[:160] + gw_rin2[...].astype(F32)).astype(BF16)
    gw_send[1, high] = term[160:].astype(BF16)
    term = gw_term(xh, yl) + gw_xin[2].astype(F32)
    gw_send[2, low] = term[:160].astype(BF16)
    gw_send[2, high] = (term[160:] + gw_lin2[...].astype(F32)).astype(BF16)
    gw_near = (copy(gw_send.at[1], gw_rin, y_right), copy(gw_send.at[2], gw_lin, y_left))

    backward(y, df)
    short_3 = out_hop(3, False, short_2)
    for qi in range(2):
        for h in range(2):
            dq_b[h, pl.ds(qi * HALF, HALF), :] = dq_t[qi, :, h * HALF:(h + 1) * HALF].T * SCALE
    dq_core = copy(dq_b.at[p], dq_in, core_peer)
    long_3 = out_hop(3, True, long_2)

    arrived(d_right[0], d_left[0])
    d_send[3, 1] = (df[over] + d_rin[1].astype(F32) + d_lin[1].astype(F32)).astype(BF16)
    d_over = copy(d_send.at[3, 1], d_x, xh_peer)

    first = c == 0

    def place(ref, mine, theirs):
        ref[:, :HEAD_DIM] = jnp.where(first, mine, theirs)
        ref[:, HEAD_DIM:] = jnp.where(first, theirs, mine)

    arrived(dq_core)
    place(dq_ref, dq_b[c], dq_in[...])
    store(1, dq_ref, dq_hbm)

    arrived(*short_3)
    for h in range(2):
        out_fin[h] = out_term(z, h) + out_in[1 - h, 3, h].astype(F32)
    arrived(*long_3)
    for h in range(2):
        out_send[0, 4, h] = (out_fin[h] + out_in[h, 3, h].astype(F32)).astype(BF16)
    pair_ici, pair_core = take(2), take()
    to_peers = [
        pltpu.make_async_remote_copy(
            src_ref=out_send.at[0, 4, h], dst_ref=out_pair_ici, send_sem=ss.at[pair_ici + h],
            recv_sem=rs.at[pair_ici], device_id=xl_peers[h], device_id_type=MESH,
        )
        for h in range(2)
    ]
    to_core = pltpu.make_async_remote_copy(
        src_ref=out_send.at[0, 4, p], dst_ref=out_pair_core, send_sem=ss.at[pair_core],
        recv_sem=rs.at[pair_core], device_id=core_peer, device_id_type=MESH,
    )

    @pl.when(same)
    def _():
        to_core.start()

    @pl.when(jnp.logical_not(same))
    def _():
        to_peers[0].start()
        to_peers[1].start()

    arrived(d_right[1], d_left[1])
    arrived(d_over)
    for part in range(2):
        total = (
            df[near, part]
            + d_rin[0, :, part].astype(F32)
            + d_lin[0, :, part].astype(F32)
            + d_x[:, part].astype(F32)
        )
        fin[:, part] = total * SCALE if part == 0 else total
    fin_core = copy(fin.at[p], fin_in, core_peer)

    arrived(*gw_near)
    gw_ref[...] = (
        gw_term(xh, y) + gw_xin[3].astype(F32) + gw_rin[...].astype(F32) + gw_lin[...].astype(F32)
    )
    store(4, gw_ref, gw_hbm)

    arrived(fin_core)
    place(dk_ref, fin[c, 0], fin_in[0])
    store(2, dk_ref, dk_hbm)
    place(dv_ref, fin[c, 1], fin_in[1])
    store(3, dv_ref, dv_hbm)

    arrived(to_peers[0])

    @pl.when(same)
    def _():
        out_ref[...] = out_send[0, 4, c].astype(F32) + out_pair_ici[...].astype(F32)
        to_core.wait_send()

    @pl.when(jnp.logical_not(same))
    def _():
        to_core.wait_recv()
        out_ref[...] = out_pair_core[...].astype(F32) + out_pair_ici[...].astype(F32)
        to_peers[0].wait_send()
        to_peers[1].wait_send()
        cot_core.wait_send()
        for pair in cot_own:
            for d in pair:
                d.wait_send()

    cot_ici.wait_send()
    for d in cot_z:
        d.wait_send()

    store(0, out_ref, out_hbm)
    for d in sent:
        d.wait_send()
    for d in stores:
        d.wait()
    assert used[0] <= SEMS, used[0]


def fused(pos, q, k, v, w, ct):
    vm = pltpu.VMEM
    scratch = [
        vm((16, 2 * TOKENS + 16, HEAD_DIM), BF16),
        vm((16, HEAD_DIM), BF16),
        vm((2, TOKENS, HEAD_DIM), BF16),
        vm((8, COLS, FEATS), BF16),
        vm((8, 2, COLS, TOKENS), BF16),
        vm((2, 1, TOKENS), F32),
        vm((2, 1, TOKENS), F32),
        vm((2, HEAD_DIM, TOKENS), F32),
        vm((2, HEAD_DIM, TOKENS), BF16),
        vm((2, 2, TOKENS, HEAD_DIM), BF16),
        vm((2, TOKENS, FEATS), BF16),
        vm((2, 2, HEAD_DIM, TOKENS), F32),
        vm((2, HEAD_DIM, TOKENS), F32),
        vm((2, HEAD_DIM, TOKENS), BF16),
        vm((2, TOKENS, HEAD_DIM), BF16),
        vm((2, 1, TOKENS), F32),
        vm((2, 5, 2, COLS, TOKENS), BF16),
        vm((2, 4, 2, COLS, TOKENS), BF16),
        vm((2, COLS, TOKENS), F32),
        vm((COLS, TOKENS), BF16),
        vm((COLS, TOKENS), BF16),
        vm((4, COLS, FEATS), BF16),
        vm((4, COLS, FEATS), BF16),
        vm((3, COLS, FEATS), BF16),
        vm((COLS // 2, FEATS), BF16),
        vm((COLS // 2, FEATS), BF16),
        vm((COLS, FEATS), BF16),
        vm((COLS, FEATS), BF16),
        vm((4, 2, TOKENS, HEAD_DIM), F32),
        vm((4, 2, TOKENS, HEAD_DIM), F32),
        vm((4, 2, 2, 2, TOKENS, HEAD_DIM), BF16),
        vm((2, 2, TOKENS, HEAD_DIM), BF16),
        vm((2, 2, TOKENS, HEAD_DIM), BF16),
        vm((2, 2, 2, TOKENS, HEAD_DIM), BF16),
        vm((2, 2, 2, TOKENS, HEAD_DIM), BF16),
        vm((2, 2, TOKENS, HEAD_DIM), BF16),
        vm((2, 2, TOKENS, HEAD_DIM), F32),
        vm((2, TOKENS, HEAD_DIM), F32),
        vm((2, HEAD_DIM, TOKENS), F32),
        vm((2, TOKENS, HEAD_DIM), F32),
        vm((TOKENS, HEAD_DIM), F32),
        pltpu.SemaphoreType.DMA((SEMS,)),
        pltpu.SemaphoreType.DMA((SEMS,)),
        pltpu.SemaphoreType.DMA((10,)),
    ]
    in_hbm = pl.BlockSpec(memory_space=pl.ANY)
    return pl.pallas_call(
        kernel,
        name="attention_core",
        out_shape=OUT_SHAPES,
        in_specs=[pl.BlockSpec(memory_space=pltpu.SMEM)] + [in_hbm] * 5,
        out_specs=(in_hbm,) * 5,
        scratch_shapes=[vm(d.shape, d.dtype) for d in OUT_SHAPES] + scratch,
        compiler_params=pltpu.CompilerParams(
            collective_id=0, has_side_effects=True, vmem_limit_bytes=62 << 20
        ),
    )(pos, q, k, v, w, ct)


OUT_SHAPES = (
    jax.ShapeDtypeStruct((COLS, TOKENS), F32),
    jax.ShapeDtypeStruct((TOKENS, FEATS), F32),
    jax.ShapeDtypeStruct((TOKENS, FEATS), F32),
    jax.ShapeDtypeStruct((TOKENS, FEATS), F32),
    jax.ShapeDtypeStruct((COLS, FEATS), F32),
)


def store_kernel(*refs):
    results, outs, held, sems = refs[:5], refs[5:10], refs[10:15], refs[15]
    loads = [pltpu.make_async_copy(results[i], held[i], sems.at[0, i]) for i in range(5)]
    stores = [pltpu.make_async_copy(held[i], outs[i], sems.at[1, i]) for i in range(5)]
    for d in loads:
        d.start()
    for load, store in zip(loads, stores):
        load.wait()
        store.start()
    for d in stores:
        d.wait()


def stored(*results):
    return pl.pallas_call(
        store_kernel,
        name="store_results",
        out_shape=OUT_SHAPES,
        in_specs=[pl.BlockSpec(memory_space=pl.ANY)] * 5,
        out_specs=(pl.BlockSpec(memory_space=pl.ANY),) * 5,
        scratch_shapes=[pltpu.VMEM(d.shape, d.dtype) for d in OUT_SHAPES]
        + [pltpu.SemaphoreType.DMA((2, 5))],
        compiler_params=pltpu.CompilerParams(vmem_limit_bytes=62 << 20),
    )(*results)


def shards(query_states, key_states, value_states, positions, out_weight, cotangent):
    results = fused(
        positions, query_states, key_states, value_states, out_weight.T, cotangent.T
    )
    out_t, grad_queries, grad_keys, grad_values, gw_t = stored(*results)
    return out_t.T, grad_queries, grad_keys, grad_values, gw_t.T


def solution(mesh):
    in_specs = (
        P("seq", "fsdp"),
        P("seq", "fsdp"),
        P("seq", "fsdp"),
        P("seq"),
        P("fsdp", "seq"),
        P("seq", "fsdp"),
    )
    out_specs = (
        P("seq", "fsdp"),
        P("seq", "fsdp"),
        P("seq", "fsdp"),
        P("seq", "fsdp"),
        P("fsdp", "seq"),
    )
    return jax.shard_map(shards, mesh=mesh, in_specs=in_specs, out_specs=out_specs, check_vma=False)
```

```python
import math

import jax
import jax.numpy as jnp
from jax import lax
from jax.experimental import pallas as pl
from jax.experimental.pallas import tpu as pltpu
from jax.sharding import PartitionSpec as P

HEAD_DIM = 128
TOKENS = 256
HALF = 128
COLS = 320
FEATS = 256
MESH = pl.DeviceIdType.MESH
BF16 = jnp.bfloat16
F32 = jnp.float32
SCALE = HEAD_DIM ** (-0.5)
SCALE_LOG2 = SCALE * math.log2(math.e)
BLOCKED = -1e30
SEMS = 112


def mm(a, b):
    return jnp.dot(a, b, preferred_element_type=F32)


def mm_nt(a, b):
    return lax.dot_general(a, b, (((1,), (1,)), ((), ())), preferred_element_type=F32)


def mm_tn(a, b):
    return lax.dot_general(a, b, (((0,), (0,)), ((), ())), preferred_element_type=F32)


def kernel(
    pos_ref, q_ref, k_ref, v_ref, w_ref, ct_ref,
    out_hbm, dq_hbm, dk_hbm, dv_hbm, gw_hbm,
    out_ref, dq_ref, dk_ref, dv_ref, gw_ref,
    kvr, res, qt, wt, cot,
    m_ref, l_ref, acc, att_t, att, att_full,
    pga, pga_in, grad_t, grad, delta,
    out_send, out_in, out_fin, out_pair_ici, out_pair_core,
    gw_xsend, gw_xin, gw_send, gw_rin2, gw_lin2, gw_rin, gw_lin,
    df, df_right, d_send, d_rin2, d_lin2, d_rin, d_lin, d_x, fin, fin_in,
    dq_t, dq_b, dq_in,
    ss, rs, ls,
):
    seq = lax.axis_index("seq")
    fsdp = lax.axis_index("fsdp")
    xh, y, c = seq // 8, (seq // 2) % 4, seq % 2
    z, xl = fsdp // 2, fsdp % 2
    p = 1 - c
    same = c == xl

    def dev(xh_, y_, c_, z_, xl_):
        return (xh_ * 8 + y_ * 2 + c_, z_ * 2 + xl_)

    yr, yl, y2 = (y + 1) % 4, (y + 3) % 4, (y + 2) % 4
    zr, zl = (z + 1) % 8, (z + 7) % 8
    core_peer = dev(xh, y, p, z, xl)
    xh_peer = dev(1 - xh, y, c, z, xl)
    y_right, y_left = dev(xh, yr, c, z, xl), dev(xh, yl, c, z, xl)
    z_right, z_left = dev(xh, y, c, zr, xl), dev(xh, y, c, zl, xl)
    xl_peers = [dev(xh, y, h, z, 1 - xl) for h in range(2)]
    xl_owner = dev(xh, y, xl, z, 1 - xl)

    used = [0]
    sent = []

    def take(count=1):
        first = used[0]
        used[0] += count
        return first

    def copy(src, dst, to):
        i = take()
        d = pltpu.make_async_remote_copy(
            src_ref=src, dst_ref=dst, send_sem=ss.at[i], recv_sem=rs.at[i],
            device_id=to, device_id_type=MESH,
        )
        d.start()
        sent.append(d)
        return d

    stores = []

    def store(i, src, dst):
        d = pltpu.make_async_copy(src, dst, ls.at[5 + i])
        d.start()
        stores.append(d)

    def arrived(*copies):
        for d in copies:
            d.wait_recv()

    own = y * 4 + xh * 2
    w_own = y * 2 + xh
    mine = pl.ds(pl.multiple_of(c * HEAD_DIM, HEAD_DIM), HEAD_DIM)
    other = pl.ds(pl.multiple_of(p * HEAD_DIM, HEAD_DIM), HEAD_DIM)
    key_rows, value_rows, res_rows = pl.ds(0, TOKENS), pl.ds(TOKENS, TOKENS), pl.ds(2 * TOKENS, 16)
    key_copy = pltpu.make_async_copy(k_ref.at[:, mine], kvr.at[own + c, key_rows], ls.at[0])
    value_copy = pltpu.make_async_copy(v_ref.at[:, mine], kvr.at[own + c, value_rows], ls.at[1])
    query_copy = pltpu.make_async_copy(q_ref.at[:, mine], qt.at[c], ls.at[2])
    weight_copy = pltpu.make_async_copy(w_ref, wt.at[w_own], ls.at[3])
    cot_copy = pltpu.make_async_copy(ct_ref, cot.at[z, c], ls.at[4])
    key_copy.start()
    value_copy.start()

    @pl.when(same)
    def _():
        cot_copy.start()

    query_copy.start()
    weight_copy.start()

    barrier = pltpu.get_barrier_semaphore()
    z_cross = [dev(xh, y, p, zr, xl), dev(xh, y, p, zl, xl)]
    xh_cross = dev(1 - xh, y, p, z, xl)
    peers = [core_peer, xh_peer, y_right, y_left, z_right, z_left] + xl_peers + z_cross + [xh_cross]
    for peer in peers:
        pl.semaphore_signal(barrier, inc=1, device_id=peer, device_id_type=MESH)
    residue = jnp.full((16, HEAD_DIM), (pos_ref[0] % 16).astype(F32)).astype(BF16)
    res[...] = residue
    kvr[own + c, res_rows, :] = residue
    key_copy.wait()
    value_copy.wait()
    pl.semaphore_wait(barrier, len(peers))

    sem_ici, sem_core, sem_z = take(2), take(), take(4)
    z_lead = dev(xh, y, xl, jnp.where(c == 0, zr, zl), xl)
    z_trail = dev(xh, y, xl, jnp.where(c == 0, zl, zr), xl)

    def cot_copy_to(h, src, to, send, recv):
        return pltpu.make_async_remote_copy(
            src_ref=src, dst_ref=cot.at[z, h], send_sem=ss.at[send], recv_sem=rs.at[recv],
            device_id=to, device_id_type=MESH,
        )

    cot_ici = cot_copy_to(c, ct_ref, xl_owner, sem_ici, sem_ici + c)
    cot_core = cot_copy_to(c, ct_ref, core_peer, sem_core, sem_core)
    cot_lead = cot_copy_to(c, ct_ref, z_lead, sem_z, sem_z + 3 * c)
    cot_trail = cot_copy_to(c, ct_ref, z_trail, sem_z + 1, sem_z + 2 - c)
    sem_own = take(4)
    cot_own = [
        [
            cot_copy_to(h, cot.at[z, h], to, sem_own + 2 * side + h, sem_z + 2 * side + h)
            for side, to in enumerate((z_right, z_left))
        ]
        for h in range(2)
    ]
    cot_ici.start()

    core_first = (
        copy(k_ref.at[:, other], kvr.at[own + c, key_rows], core_peer),
        copy(v_ref.at[:, other], kvr.at[own + c, value_rows], core_peer),
        copy(res, kvr.at[own + c, res_rows], core_peer),
    )

    def kv_send(slot, *targets):
        block = kvr.at[slot]
        return [copy(block, block, to) for to in targets]

    kv_c = kv_send(own + c, y_right, y_left, xh_peer)
    cot_lead.start()

    @pl.when(jnp.logical_not(same))
    def _():
        cot_core.start()

    w_right = copy(w_ref, wt.at[w_own], y_right)
    w_left = copy(w_ref, wt.at[w_own], y_left)
    q_core = copy(q_ref.at[:, other], qt.at[c], core_peer)

    def z_pair(right_slot, left_slot, lead):
        a = cot.at[right_slot % 8, 0 if lead else 1]
        b = cot.at[left_slot % 8, 1 if lead else 0]
        return copy(a, a, z_right), copy(b, b, z_left)

    arrived(*core_first)
    kv_p = kv_send(own + p, y_right, y_left, xh_peer)
    cot_trail.start()

    @pl.when(same)
    def _():
        cot_copy.wait()
        cot_core.wait_recv()

    @pl.when(jnp.logical_not(same))
    def _():
        for h in range(2):
            cot_copy_to(h, ct_ref, xl_owner, sem_ici, sem_ici + h).wait_recv()
        cot_own[0][0].start()
        cot_own[1][1].start()

    w_xh = [copy(w_ref, wt.at[w_own], xh_peer)]

    acc[...] = jnp.zeros_like(acc)
    l_ref[...] = jnp.zeros_like(l_ref)
    m_ref[...] = jnp.full_like(m_ref, BLOCKED)
    pga[...] = jnp.zeros_like(pga)
    dq_t[...] = jnp.zeros_like(dq_t)
    query_copy.wait()
    weight_copy.wait()
    arrived(q_core)

    kv_far = []
    over_own = y * 4 + (1 - xh) * 2

    arrived(kv_c[0])
    kv_far += kv_send(yl * 4 + xh * 2 + c, y_right)
    arrived(kv_c[1], kv_c[2])
    kv_over_c = kv_send(over_own + c, y_right, y_left)

    @pl.when(jnp.logical_not(same))
    def _():
        cot_own[1][0].start()
        cot_own[0][1].start()

    arrived(cot_own[0][0], cot_own[1][1])
    z_lead_two = z_pair(z + 7, z + 1, True)
    arrived(w_right, w_left)
    w_low, w_high = wt.at[yl * 2 + xh, pl.ds(0, 160)], wt.at[yr * 2 + xh, pl.ds(160, 160)]
    w_far = (copy(w_low, w_low, y_right), copy(w_high, w_high, y_left))
    w_xh.append(copy(wt.at[yl * 2 + xh], wt.at[yl * 2 + xh], xh_peer))
    w_xh.append(copy(wt.at[yr * 2 + xh], wt.at[yr * 2 + xh], xh_peer))
    arrived(cot_own[1][0], cot_own[0][1])
    z_trail_two = z_pair(z + 7, z + 1, False)
    arrived(*kv_p)
    kv_over_p = kv_send(over_own + p, y_right, y_left)
    kv_far += kv_send(yr * 4 + xh * 2 + p, y_left)

    ahead = (
        lax.broadcasted_iota(jnp.int32, (1, HALF, TOKENS), 2) % HALF
        - lax.broadcasted_iota(jnp.int32, (1, HALF, TOKENS), 1)
    )

    def residue_rows(slot, count):
        return kvr[pl.ds(slot, count), pl.ds(2 * TOKENS, 16), :].astype(F32)[:, 0:1, :]

    query_res = residue_rows(own, 2)
    query_res = jnp.concatenate([query_res[0:1], query_res[1:2]], axis=2)

    def tile_scores(yy, qi, ki):
        key_res = residue_rows(yy * 4, 4)
        key_res = jnp.concatenate([key_res, key_res], axis=2)
        bound = jnp.where(key_res <= query_res, 0, 1) - jnp.where(qi > ki, 4 * HALF, 0)
        rows = pl.multiple_of(ki * HALF, HALF)
        keys = kvr[pl.ds(yy * 4, 4), pl.ds(rows, HALF), :].reshape(4 * HALF, HEAD_DIM)
        values = kvr[pl.ds(yy * 4, 4), pl.ds(TOKENS + rows, HALF), :].reshape(4 * HALF, HEAD_DIM)
        query_rows = pl.ds(pl.multiple_of(qi * HALF, HALF), HALF)
        queries = qt[:, query_rows, :].reshape(TOKENS, HEAD_DIM)
        scores = mm_nt(keys, queries) * SCALE_LOG2
        seen = ahead >= bound
        scores = jnp.where(seen, scores.reshape(4, HALF, TOKENS), BLOCKED)
        return scores.reshape(4 * HALF, TOKENS), keys, values, queries

    def forward(yy):
        def tile(t, carry):
            qi, ki = (t + 1) // 2, t // 2
            scores, _, values, _ = tile_scores(yy, qi, ki)
            old = m_ref[qi]
            new = jnp.maximum(old, jnp.max(scores, axis=0, keepdims=True))
            probs = jnp.exp2(scores - new)
            shrink = jnp.exp2(old - new)
            m_ref[qi] = new
            l_ref[qi] = l_ref[qi] * shrink + jnp.sum(probs, axis=0, keepdims=True)
            acc[qi] = acc[qi] * shrink + mm_tn(values, probs.astype(BF16))
            return carry

        lax.fori_loop(0, 3, tile, 0)

    forward(y)
    arrived(*z_lead_two)
    z_lead_three = z_pair(z + 6, z + 2, True)
    arrived(*kv_over_c)
    kv_far += kv_send(yl * 4 + (1 - xh) * 2 + c, y_right)
    arrived(*w_far)
    w_xh.append(copy(wt.at[y2 * 2 + xh], wt.at[y2 * 2 + xh], xh_peer))
    arrived(*z_trail_two)
    z_trail_three = z_pair(z + 6, z + 2, False)
    arrived(*kv_over_p)
    kv_far += kv_send(yr * 4 + (1 - xh) * 2 + p, y_left)
    forward(yl)
    arrived(*z_lead_three)
    z_four = z_pair(z + 5, z + 3, True)
    forward(yr)
    arrived(*kv_far)
    forward(y2)

    for qi in range(2):
        total = l_ref[qi]
        rows = (acc[qi] / total).astype(BF16)
        att_t[qi] = rows
        m_ref[qi] = m_ref[qi] + jnp.log2(total)
        wide = rows.astype(F32)
        for h in range(2):
            att[c, h, pl.ds(qi * HALF, HALF), :] = wide[:, h * HALF:(h + 1) * HALF].T.astype(BF16)
    att_core = copy(att.at[c], att.at[c], core_peer)
    arrived(*w_xh)
    arrived(*z_trail_three)

    def w_block(i):
        return wt[(i % 4) * 2 + i // 4]

    def width_step(k, carry):
        i = (z + 5 + k) % 8
        weight = w_block(i)
        for h in range(2):
            term = mm_tn(weight, cot[i, h])
            pga[0, h] += term[:HEAD_DIM]
            pga[1, h] += term[HEAD_DIM:]
        return carry

    lax.fori_loop(0, 7, width_step, 0)
    arrived(att_core)
    for h in range(2):
        att_full[h] = jnp.concatenate([att[0, h], att[1, h]], axis=1)

    def out_term(i, h):
        return mm_nt(w_block(i), att_full[h])

    def out_hop(step, long_chain, got):
        sends = []
        for side in range(2):
            h = side if long_chain else 1 - side
            target = (z + 4 - step) % 8 if side == 0 else (z + 4 + step) % 8
            term = out_term(target, h)
            if got is not None:
                arrived(got[side])
                term = term + out_in[side, step - 1, h].astype(F32)
            out_send[side, step, h] = term.astype(BF16)
            sends.append(
                copy(out_send.at[side, step, h], out_in.at[side, step, h], z_left if side else z_right)
            )
        return sends

    long_0 = out_hop(0, True, None)
    arrived(*z_four)

    width_step(7, 0)
    pga_core = copy(pga.at[p], pga_in, core_peer)
    short_1 = out_hop(1, False, None)

    def gw_term(x, yy):
        i = x * 4 + yy
        return mm(cot[i, 0], att_full[0]) + mm(cot[i, 1], att_full[1])

    gw_over = []
    for i, yy in enumerate((y2, yr, yl, y)):
        gw_xsend[i] = gw_term(1 - xh, yy).astype(BF16)
        gw_over.append(copy(gw_xsend.at[i], gw_xin.at[i], xh_peer))

    arrived(pga_core)
    for h in range(2):
        rows = (pga[c, h] + pga_in[h]).astype(BF16)
        for qi in range(2):
            grad_t[qi, :, h * HALF:(h + 1) * HALF] = rows[:, qi * HALF:(qi + 1) * HALF]
    for qi in range(2):
        wide = grad_t[qi].astype(F32)
        delta[qi] = jnp.sum(wide * att_t[qi].astype(F32), axis=0, keepdims=True)
        grad[qi] = wide.T.astype(BF16)

    def backward(yy, df):
        df[...] = jnp.zeros_like(df)

        def tile(t, carry):
            qi, ki = (t + 1) // 2, t // 2
            scores, keys, values, queries = tile_scores(yy, qi, ki)
            probs = jnp.exp2(scores - m_ref[qi])
            grad_probs = mm(values, grad_t[qi])
            grad_scores = (probs * (grad_probs - delta[qi])).astype(BF16)
            rows = pl.ds(pl.multiple_of(ki * HALF, HALF), HALF)
            grad_keys = mm(grad_scores, queries).reshape(4, HALF, HEAD_DIM)
            grad_values = mm(probs.astype(BF16), grad[qi]).reshape(4, HALF, HEAD_DIM)
            df[:, 0, rows, :] += grad_keys
            df[:, 1, rows, :] += grad_values
            dq_t[qi] += mm_tn(keys, grad_scores)
            return carry

        lax.fori_loop(0, 3, tile, 0)

    near = pl.ds(2 * xh, 2)
    over = pl.ds(2 * (1 - xh), 2)

    backward(y2, df)
    d_send[0, 0] = df[near].astype(BF16)
    d_far_right = copy(d_send.at[0, 0], d_rin2, y_right)
    d_send[0, 1] = df[over].astype(BF16)
    d_far_left = copy(d_send.at[0, 1], d_lin2, y_left)
    long_1 = out_hop(1, True, long_0)

    arrived(gw_over[0])
    gw_send[0] = (gw_term(xh, y2) + gw_xin[0].astype(F32)).astype(BF16)
    gw_far = (
        copy(gw_send.at[0, pl.ds(0, 160)], gw_rin2, y_right),
        copy(gw_send.at[0, pl.ds(160, 160)], gw_lin2, y_left),
    )

    backward(yr, df_right)
    d_send[1, 1] = df_right[over].astype(BF16)
    d_right = [copy(d_send.at[1, 1], d_rin.at[1], y_right)]
    short_2 = out_hop(2, False, short_1)
    backward(yl, df)
    arrived(d_far_left)
    d_send[2, 1] = (df[over] + d_lin2[...].astype(F32)).astype(BF16)
    d_left = [copy(d_send.at[2, 1], d_lin.at[1], y_left)]
    arrived(d_far_right)
    d_send[1, 0] = (df_right[near] + d_rin2[...].astype(F32)).astype(BF16)
    d_right.append(copy(d_send.at[1, 0], d_rin.at[0], y_right))
    d_send[2, 0] = df[near].astype(BF16)
    d_left.append(copy(d_send.at[2, 0], d_lin.at[0], y_left))
    long_2 = out_hop(2, True, long_1)

    arrived(*gw_far)
    arrived(*gw_over[1:])
    low, high = pl.ds(0, 160), pl.ds(160, 160)
    term = gw_term(xh, yr) + gw_xin[1].astype(F32)
    gw_send[1, low] = (term[:160] + gw_rin2[...].astype(F32)).astype(BF16)
    gw_send[1, high] = term[160:].astype(BF16)
    term = gw_term(xh, yl) + gw_xin[2].astype(F32)
    gw_send[2, low] = term[:160].astype(BF16)
    gw_send[2, high] = (term[160:] + gw_lin2[...].astype(F32)).astype(BF16)
    gw_near = (copy(gw_send.at[1], gw_rin, y_right), copy(gw_send.at[2], gw_lin, y_left))

    backward(y, df)
    short_3 = out_hop(3, False, short_2)
    for qi in range(2):
        for h in range(2):
            dq_b[h, pl.ds(qi * HALF, HALF), :] = dq_t[qi, :, h * HALF:(h + 1) * HALF].T * SCALE
    dq_core = copy(dq_b.at[p], dq_in, core_peer)
    long_3 = out_hop(3, True, long_2)

    arrived(d_right[0], d_left[0])
    d_send[3, 1] = (df[over] + d_rin[1].astype(F32) + d_lin[1].astype(F32)).astype(BF16)
    sem_d = take(2)
    d_over = [
        pltpu.make_async_remote_copy(
            src_ref=d_send.at[3, 1, h], dst_ref=d_x.at[c], send_sem=ss.at[sem_d + i],
            recv_sem=rs.at[sem_d + i], device_id=to, device_id_type=MESH,
        )
        for i, (h, to) in enumerate(((c, xh_peer), (p, xh_cross)))
    ]
    for d in d_over:
        d.start()
    sent.extend(d_over)

    first = c == 0

    def place(ref, mine, theirs):
        ref[:, :HEAD_DIM] = jnp.where(first, mine, theirs)
        ref[:, HEAD_DIM:] = jnp.where(first, theirs, mine)

    arrived(dq_core)
    place(dq_ref, dq_b[c], dq_in[...])
    store(1, dq_ref, dq_hbm)

    arrived(*short_3)
    for h in range(2):
        out_fin[h] = out_term(z, h) + out_in[1 - h, 3, h].astype(F32)
    gw_ref[...] = gw_term(xh, y) + gw_xin[3].astype(F32)

    arrived(d_right[1], d_left[1])
    for part in range(2):
        total = df[near, part] + d_rin[0, :, part].astype(F32) + d_lin[0, :, part].astype(F32)
        fin[:, part] = total
    fin_core = copy(fin.at[p], fin_in, core_peer)

    arrived(*long_3)
    for h in range(2):
        out_send[0, 4, h] = (out_fin[h] + out_in[h, 3, h].astype(F32)).astype(BF16)
    pair_ici, pair_core = take(2), take()
    to_peers = [
        pltpu.make_async_remote_copy(
            src_ref=out_send.at[0, 4, h], dst_ref=out_pair_ici, send_sem=ss.at[pair_ici + h],
            recv_sem=rs.at[pair_ici], device_id=xl_peers[h], device_id_type=MESH,
        )
        for h in range(2)
    ]
    to_core = pltpu.make_async_remote_copy(
        src_ref=out_send.at[0, 4, p], dst_ref=out_pair_core, send_sem=ss.at[pair_core],
        recv_sem=rs.at[pair_core], device_id=core_peer, device_id_type=MESH,
    )

    @pl.when(same)
    def _():
        to_core.start()

    @pl.when(jnp.logical_not(same))
    def _():
        to_peers[0].start()
        to_peers[1].start()

    arrived(*gw_near)
    gw_ref[...] += gw_rin[...].astype(F32) + gw_lin[...].astype(F32)
    store(4, gw_ref, gw_hbm)

    arrived(fin_core, *d_over)
    for i, (ref, factor) in enumerate(((dk_ref, SCALE), (dv_ref, 1.0))):
        mine = (fin[c, i] + d_x[c, i].astype(F32)) * factor
        theirs = (fin_in[i] + d_x[p, i].astype(F32)) * factor
        place(ref, mine, theirs)
        store(2 + i, ref, (dk_hbm, dv_hbm)[i])

    arrived(to_peers[0])

    @pl.when(same)
    def _():
        out_ref[...] = out_send[0, 4, c].astype(F32) + out_pair_ici[...].astype(F32)
        to_core.wait_send()

    @pl.when(jnp.logical_not(same))
    def _():
        to_core.wait_recv()
        out_ref[...] = out_pair_core[...].astype(F32) + out_pair_ici[...].astype(F32)
        to_peers[0].wait_send()
        to_peers[1].wait_send()
        cot_core.wait_send()
        for pair in cot_own:
            for d in pair:
                d.wait_send()

    cot_ici.wait_send()
    cot_lead.wait_send()
    cot_trail.wait_send()

    store(0, out_ref, out_hbm)
    for d in sent:
        d.wait_send()
    for d in stores:
        d.wait()
    assert used[0] <= SEMS, used[0]


def fused(pos, q, k, v, w, ct):
    vm = pltpu.VMEM
    scratch = [
        vm((16, 2 * TOKENS + 16, HEAD_DIM), BF16),
        vm((16, HEAD_DIM), BF16),
        vm((2, TOKENS, HEAD_DIM), BF16),
        vm((8, COLS, FEATS), BF16),
        vm((8, 2, COLS, TOKENS), BF16),
        vm((2, 1, TOKENS), F32),
        vm((2, 1, TOKENS), F32),
        vm((2, HEAD_DIM, TOKENS), F32),
        vm((2, HEAD_DIM, TOKENS), BF16),
        vm((2, 2, TOKENS, HEAD_DIM), BF16),
        vm((2, TOKENS, FEATS), BF16),
        vm((2, 2, HEAD_DIM, TOKENS), F32),
        vm((2, HEAD_DIM, TOKENS), F32),
        vm((2, HEAD_DIM, TOKENS), BF16),
        vm((2, TOKENS, HEAD_DIM), BF16),
        vm((2, 1, TOKENS), F32),
        vm((2, 5, 2, COLS, TOKENS), BF16),
        vm((2, 4, 2, COLS, TOKENS), BF16),
        vm((2, COLS, TOKENS), F32),
        vm((COLS, TOKENS), BF16),
        vm((COLS, TOKENS), BF16),
        vm((4, COLS, FEATS), BF16),
        vm((4, COLS, FEATS), BF16),
        vm((3, COLS, FEATS), BF16),
        vm((COLS // 2, FEATS), BF16),
        vm((COLS // 2, FEATS), BF16),
        vm((COLS, FEATS), BF16),
        vm((COLS, FEATS), BF16),
        vm((4, 2, TOKENS, HEAD_DIM), F32),
        vm((4, 2, TOKENS, HEAD_DIM), F32),
        vm((4, 2, 2, 2, TOKENS, HEAD_DIM), BF16),
        vm((2, 2, TOKENS, HEAD_DIM), BF16),
        vm((2, 2, TOKENS, HEAD_DIM), BF16),
        vm((2, 2, 2, TOKENS, HEAD_DIM), BF16),
        vm((2, 2, 2, TOKENS, HEAD_DIM), BF16),
        vm((2, 2, TOKENS, HEAD_DIM), BF16),
        vm((2, 2, TOKENS, HEAD_DIM), F32),
        vm((2, TOKENS, HEAD_DIM), F32),
        vm((2, HEAD_DIM, TOKENS), F32),
        vm((2, TOKENS, HEAD_DIM), F32),
        vm((TOKENS, HEAD_DIM), F32),
        pltpu.SemaphoreType.DMA((SEMS,)),
        pltpu.SemaphoreType.DMA((SEMS,)),
        pltpu.SemaphoreType.DMA((10,)),
    ]
    in_hbm = pl.BlockSpec(memory_space=pl.ANY)
    return pl.pallas_call(
        kernel,
        name="attention_core",
        out_shape=OUT_SHAPES,
        in_specs=[pl.BlockSpec(memory_space=pltpu.SMEM)] + [in_hbm] * 5,
        out_specs=(in_hbm,) * 5,
        scratch_shapes=[vm(d.shape, d.dtype) for d in OUT_SHAPES] + scratch,
        compiler_params=pltpu.CompilerParams(
            collective_id=0, has_side_effects=True, vmem_limit_bytes=62 << 20
        ),
    )(pos, q, k, v, w, ct)


OUT_SHAPES = (
    jax.ShapeDtypeStruct((COLS, TOKENS), F32),
    jax.ShapeDtypeStruct((TOKENS, FEATS), F32),
    jax.ShapeDtypeStruct((TOKENS, FEATS), F32),
    jax.ShapeDtypeStruct((TOKENS, FEATS), F32),
    jax.ShapeDtypeStruct((COLS, FEATS), F32),
)


def store_kernel(*refs):
    results, outs, held, sems = refs[:5], refs[5:10], refs[10:15], refs[15]
    loads = [pltpu.make_async_copy(results[i], held[i], sems.at[0, i]) for i in range(5)]
    stores = [pltpu.make_async_copy(held[i], outs[i], sems.at[1, i]) for i in range(5)]
    for d in loads:
        d.start()
    for load, store in zip(loads, stores):
        load.wait()
        store.start()
    for d in stores:
        d.wait()


def stored(*results):
    return pl.pallas_call(
        store_kernel,
        name="store_results",
        out_shape=OUT_SHAPES,
        in_specs=[pl.BlockSpec(memory_space=pl.ANY)] * 5,
        out_specs=(pl.BlockSpec(memory_space=pl.ANY),) * 5,
        scratch_shapes=[pltpu.VMEM(d.shape, d.dtype) for d in OUT_SHAPES]
        + [pltpu.SemaphoreType.DMA((2, 5))],
        compiler_params=pltpu.CompilerParams(vmem_limit_bytes=62 << 20),
    )(*results)


def shards(query_states, key_states, value_states, positions, out_weight, cotangent):
    results = fused(
        positions, query_states, key_states, value_states, out_weight.T, cotangent.T
    )
    out_t, grad_queries, grad_keys, grad_values, gw_t = stored(*results)
    return out_t.T, grad_queries, grad_keys, grad_values, gw_t.T


def solution(mesh):
    in_specs = (
        P("seq", "fsdp"),
        P("seq", "fsdp"),
        P("seq", "fsdp"),
        P("seq"),
        P("fsdp", "seq"),
        P("seq", "fsdp"),
    )
    out_specs = (
        P("seq", "fsdp"),
        P("seq", "fsdp"),
        P("seq", "fsdp"),
        P("seq", "fsdp"),
        P("fsdp", "seq"),
    )
    return jax.shard_map(shards, mesh=mesh, in_specs=in_specs, out_specs=out_specs, check_vma=False)
```

```python
import math

import jax
import jax.numpy as jnp
from jax import lax
from jax.experimental import pallas as pl
from jax.experimental.pallas import tpu as pltpu
from jax.sharding import PartitionSpec as P

HEAD_DIM = 128
TOKENS = 256
HALF = 128
COLS = 320
FEATS = 256
MESH = pl.DeviceIdType.MESH
BF16 = jnp.bfloat16
F32 = jnp.float32
SCALE = HEAD_DIM ** (-0.5)
SCALE_LOG2 = SCALE * math.log2(math.e)
BLOCKED = -1e30
SEMS = 112


def mm(a, b):
    return jnp.dot(a, b, preferred_element_type=F32)


def mm_nt(a, b):
    return lax.dot_general(a, b, (((1,), (1,)), ((), ())), preferred_element_type=F32)


def mm_tn(a, b):
    return lax.dot_general(a, b, (((0,), (0,)), ((), ())), preferred_element_type=F32)


def kernel(
    pos_ref, q_ref, k_ref, v_ref, w_ref, ct_ref,
    out_hbm, dq_hbm, dk_hbm, dv_hbm, gw_hbm,
    out_ref, dq_ref, dk_ref, dv_ref, gw_ref,
    kvr, res, qt, wt, cot,
    m_ref, l_ref, acc, att_t, att, att_full,
    pga, pga_in, grad_t, grad, delta,
    out_send, out_in, out_fin, out_pair_ici, out_pair_core,
    gw_xsend, gw_xin, gw_send, gw_rin2, gw_lin2, gw_rin, gw_lin,
    df, df_right, d_send, d_rin2, d_lin2, d_rin, d_lin, d_x, fin, fin_in,
    dq_t, dq_b, dq_in,
    ss, rs, ls,
):
    seq = lax.axis_index("seq")
    fsdp = lax.axis_index("fsdp")
    xh, y, c = seq // 8, (seq // 2) % 4, seq % 2
    z, xl = fsdp // 2, fsdp % 2
    p = 1 - c
    same = c == xl

    def dev(xh_, y_, c_, z_, xl_):
        return (xh_ * 8 + y_ * 2 + c_, z_ * 2 + xl_)

    yr, yl, y2 = (y + 1) % 4, (y + 3) % 4, (y + 2) % 4
    zr, zl = (z + 1) % 8, (z + 7) % 8
    core_peer = dev(xh, y, p, z, xl)
    xh_peer = dev(1 - xh, y, c, z, xl)
    y_right, y_left = dev(xh, yr, c, z, xl), dev(xh, yl, c, z, xl)
    z_right, z_left = dev(xh, y, c, zr, xl), dev(xh, y, c, zl, xl)
    xl_peers = [dev(xh, y, h, z, 1 - xl) for h in range(2)]
    xl_owner = dev(xh, y, xl, z, 1 - xl)

    used = [0]
    sent = []

    def take(count=1):
        first = used[0]
        used[0] += count
        return first

    def copy(src, dst, to):
        i = take()
        d = pltpu.make_async_remote_copy(
            src_ref=src, dst_ref=dst, send_sem=ss.at[i], recv_sem=rs.at[i],
            device_id=to, device_id_type=MESH,
        )
        d.start()
        sent.append(d)
        return d

    stores = []

    def store(i, src, dst):
        d = pltpu.make_async_copy(src, dst, ls.at[5 + i])
        d.start()
        stores.append(d)

    def arrived(*copies):
        for d in copies:
            d.wait_recv()

    own = y * 4 + xh * 2
    w_own = y * 2 + xh
    mine = pl.ds(pl.multiple_of(c * HEAD_DIM, HEAD_DIM), HEAD_DIM)
    other = pl.ds(pl.multiple_of(p * HEAD_DIM, HEAD_DIM), HEAD_DIM)
    key_rows, value_rows, res_rows = pl.ds(0, TOKENS), pl.ds(TOKENS, TOKENS), pl.ds(2 * TOKENS, 16)
    key_copy = pltpu.make_async_copy(k_ref.at[:, mine], kvr.at[own + c, key_rows], ls.at[0])
    value_copy = pltpu.make_async_copy(v_ref.at[:, mine], kvr.at[own + c, value_rows], ls.at[1])
    query_copy = pltpu.make_async_copy(q_ref.at[:, mine], qt.at[c], ls.at[2])
    weight_copy = pltpu.make_async_copy(w_ref, wt.at[w_own], ls.at[3])
    cot_copy = pltpu.make_async_copy(ct_ref, cot.at[z, c], ls.at[4])
    key_copy.start()
    value_copy.start()

    @pl.when(same)
    def _():
        cot_copy.start()

    query_copy.start()
    weight_copy.start()

    barrier = pltpu.get_barrier_semaphore()
    z_cross = [dev(xh, y, p, zr, xl), dev(xh, y, p, zl, xl)]
    xh_cross = dev(1 - xh, y, p, z, xl)
    peers = [core_peer, xh_peer, y_right, y_left, z_right, z_left] + xl_peers + z_cross + [xh_cross]
    for peer in peers:
        pl.semaphore_signal(barrier, inc=1, device_id=peer, device_id_type=MESH)
    residue = jnp.full((16, HEAD_DIM), (pos_ref[0] % 16).astype(F32)).astype(BF16)
    res[...] = residue
    kvr[own + c, res_rows, :] = residue
    key_copy.wait()
    value_copy.wait()
    pl.semaphore_wait(barrier, len(peers))

    sem_ici, sem_core, sem_z = take(2), take(), take(4)
    z_lead = dev(xh, y, xl, jnp.where(c == 0, zr, zl), xl)
    z_trail = dev(xh, y, xl, jnp.where(c == 0, zl, zr), xl)

    def cot_copy_to(h, src, to, send, recv):
        return pltpu.make_async_remote_copy(
            src_ref=src, dst_ref=cot.at[z, h], send_sem=ss.at[send], recv_sem=rs.at[recv],
            device_id=to, device_id_type=MESH,
        )

    cot_ici = cot_copy_to(c, ct_ref, xl_owner, sem_ici, sem_ici + c)
    cot_core = cot_copy_to(c, ct_ref, core_peer, sem_core, sem_core)
    cot_lead = cot_copy_to(c, ct_ref, z_lead, sem_z, sem_z + 3 * c)
    cot_trail = cot_copy_to(c, ct_ref, z_trail, sem_z + 1, sem_z + 2 - c)
    sem_own = take(4)
    cot_own = [
        [
            cot_copy_to(h, cot.at[z, h], to, sem_own + 2 * side + h, sem_z + 2 * side + h)
            for side, to in enumerate((z_right, z_left))
        ]
        for h in range(2)
    ]
    cot_ici.start()

    core_first = (
        copy(k_ref.at[:, other], kvr.at[own + c, key_rows], core_peer),
        copy(v_ref.at[:, other], kvr.at[own + c, value_rows], core_peer),
        copy(res, kvr.at[own + c, res_rows], core_peer),
    )

    def kv_send(slot, *targets):
        block = kvr.at[slot]
        return [copy(block, block, to) for to in targets]

    kv_c = kv_send(own + c, y_right, y_left, xh_peer)
    cot_lead.start()

    @pl.when(jnp.logical_not(same))
    def _():
        cot_core.start()

    w_right = copy(w_ref, wt.at[w_own], y_right)
    w_left = copy(w_ref, wt.at[w_own], y_left)
    q_core = copy(q_ref.at[:, other], qt.at[c], core_peer)

    def z_pair(right_slot, left_slot, lead):
        a = cot.at[right_slot % 8, 0 if lead else 1]
        b = cot.at[left_slot % 8, 1 if lead else 0]
        return copy(a, a, z_right), copy(b, b, z_left)

    arrived(*core_first)
    kv_p = kv_send(own + p, y_right, y_left, xh_peer)
    cot_trail.start()

    @pl.when(same)
    def _():
        cot_copy.wait()
        cot_core.wait_recv()

    @pl.when(jnp.logical_not(same))
    def _():
        for h in range(2):
            cot_copy_to(h, ct_ref, xl_owner, sem_ici, sem_ici + h).wait_recv()
        cot_own[0][0].start()
        cot_own[1][1].start()

    w_xh = [copy(w_ref, wt.at[w_own], xh_peer)]

    acc[...] = jnp.zeros_like(acc)
    l_ref[...] = jnp.zeros_like(l_ref)
    m_ref[...] = jnp.full_like(m_ref, BLOCKED)
    pga[...] = jnp.zeros_like(pga)
    dq_t[...] = jnp.zeros_like(dq_t)
    query_copy.wait()
    weight_copy.wait()
    arrived(q_core)

    kv_far = []
    over_own = y * 4 + (1 - xh) * 2

    arrived(kv_c[0])
    kv_far += kv_send(yl * 4 + xh * 2 + c, y_right)
    arrived(kv_c[1], kv_c[2])
    kv_over_c = kv_send(over_own + c, y_right, y_left)

    @pl.when(jnp.logical_not(same))
    def _():
        cot_own[1][0].start()
        cot_own[0][1].start()

    arrived(cot_own[0][0], cot_own[1][1])
    z_lead_two = z_pair(z + 7, z + 1, True)
    arrived(w_right, w_left)
    w_low, w_high = wt.at[yl * 2 + xh, pl.ds(0, 160)], wt.at[yr * 2 + xh, pl.ds(160, 160)]
    w_far = (copy(w_low, w_low, y_right), copy(w_high, w_high, y_left))
    w_xh.append(copy(wt.at[yl * 2 + xh], wt.at[yl * 2 + xh], xh_peer))
    w_xh.append(copy(wt.at[yr * 2 + xh], wt.at[yr * 2 + xh], xh_peer))
    arrived(cot_own[1][0], cot_own[0][1])
    z_trail_two = z_pair(z + 7, z + 1, False)
    arrived(*kv_p)
    kv_over_p = kv_send(over_own + p, y_right, y_left)
    kv_far += kv_send(yr * 4 + xh * 2 + p, y_left)

    ahead = (
        lax.broadcasted_iota(jnp.int32, (1, HALF, TOKENS), 2) % HALF
        - lax.broadcasted_iota(jnp.int32, (1, HALF, TOKENS), 1)
    )

    def residue_rows(slot, count):
        return kvr[pl.ds(slot, count), pl.ds(2 * TOKENS, 16), :].astype(F32)[:, 0:1, :]

    query_res = residue_rows(own, 2)
    query_res = jnp.concatenate([query_res[0:1], query_res[1:2]], axis=2)

    def tile_scores(yy, qi, ki):
        key_res = residue_rows(yy * 4, 4)
        key_res = jnp.concatenate([key_res, key_res], axis=2)
        bound = jnp.where(key_res <= query_res, 0, 1) - jnp.where(qi > ki, 4 * HALF, 0)
        rows = pl.multiple_of(ki * HALF, HALF)
        keys = kvr[pl.ds(yy * 4, 4), pl.ds(rows, HALF), :].reshape(4 * HALF, HEAD_DIM)
        values = kvr[pl.ds(yy * 4, 4), pl.ds(TOKENS + rows, HALF), :].reshape(4 * HALF, HEAD_DIM)
        query_rows = pl.ds(pl.multiple_of(qi * HALF, HALF), HALF)
        queries = qt[:, query_rows, :].reshape(TOKENS, HEAD_DIM)
        scores = mm_nt(keys, queries) * SCALE_LOG2
        seen = ahead >= bound
        scores = jnp.where(seen, scores.reshape(4, HALF, TOKENS), BLOCKED)
        return scores.reshape(4 * HALF, TOKENS), keys, values, queries

    def forward(yy):
        def tile(t, carry):
            qi, ki = (t + 1) // 2, t // 2
            scores, _, values, _ = tile_scores(yy, qi, ki)
            old = m_ref[qi]
            new = jnp.maximum(old, jnp.max(scores, axis=0, keepdims=True))
            probs = jnp.exp2(scores - new)
            shrink = jnp.exp2(old - new)
            m_ref[qi] = new
            l_ref[qi] = l_ref[qi] * shrink + jnp.sum(probs, axis=0, keepdims=True)
            acc[qi] = acc[qi] * shrink + mm_tn(values, probs.astype(BF16))
            return carry

        lax.fori_loop(0, 3, tile, 0)

    forward(y)
    arrived(*z_lead_two)
    z_lead_three = z_pair(z + 6, z + 2, True)
    arrived(*kv_over_c)
    kv_far += kv_send(yl * 4 + (1 - xh) * 2 + c, y_right)
    arrived(*w_far)
    w_xh.append(copy(wt.at[y2 * 2 + xh], wt.at[y2 * 2 + xh], xh_peer))
    arrived(*z_trail_two)
    z_trail_three = z_pair(z + 6, z + 2, False)
    arrived(*kv_over_p)
    kv_far += kv_send(yr * 4 + (1 - xh) * 2 + p, y_left)
    forward(yl)
    arrived(*z_lead_three)
    z_four = z_pair(z + 5, z + 3, True)
    forward(yr)
    arrived(*kv_far)
    forward(y2)

    for qi in range(2):
        total = l_ref[qi]
        rows = (acc[qi] / total).astype(BF16)
        att_t[qi] = rows
        m_ref[qi] = m_ref[qi] + jnp.log2(total)
        wide = rows.astype(F32)
        for h in range(2):
            att[c, h, pl.ds(qi * HALF, HALF), :] = wide[:, h * HALF:(h + 1) * HALF].T.astype(BF16)
    att_core = copy(att.at[c], att.at[c], core_peer)
    arrived(*w_xh)
    arrived(*z_trail_three)

    def w_block(i):
        return wt[(i % 4) * 2 + i // 4]

    def width_step(k, carry):
        i = (z + 5 + k) % 8
        weight = w_block(i)
        for h in range(2):
            term = mm_tn(weight, cot[i, h])
            pga[0, h] += term[:HEAD_DIM]
            pga[1, h] += term[HEAD_DIM:]
        return carry

    lax.fori_loop(0, 7, width_step, 0)
    arrived(att_core)
    for h in range(2):
        att_full[h] = jnp.concatenate([att[0, h], att[1, h]], axis=1)

    def out_term(i, h):
        return mm_nt(w_block(i), att_full[h])

    def out_hop(step, long_chain, got):
        sends = []
        halves = (0, 1) if long_chain else (1, 0)
        targets = ((z + 4 - step) % 8, (z + 4 + step) % 8)
        terms = [out_term(targets[side], halves[side]) for side in range(2)]
        for side, h in enumerate(halves):
            term = terms[side]
            if got is not None:
                arrived(got[side])
                term = term + out_in[side, step - 1, h].astype(F32)
            out_send[side, step, h] = term.astype(BF16)
            sends.append(
                copy(out_send.at[side, step, h], out_in.at[side, step, h], z_left if side else z_right)
            )
        return sends

    long_0 = out_hop(0, True, None)
    arrived(*z_four)

    width_step(7, 0)
    pga_core = copy(pga.at[p], pga_in, core_peer)

    def gw_term(x, yy):
        i = x * 4 + yy
        return mm(cot[i, 0], att_full[0]) + mm(cot[i, 1], att_full[1])

    gw_over = []
    for i, yy in enumerate((y2, yr, yl, y)):
        gw_xsend[i] = gw_term(1 - xh, yy).astype(BF16)
        gw_over.append(copy(gw_xsend.at[i], gw_xin.at[i], xh_peer))

    short_1 = out_hop(1, False, None)
    arrived(pga_core)
    for h in range(2):
        rows = (pga[c, h] + pga_in[h]).astype(BF16)
        for qi in range(2):
            grad_t[qi, :, h * HALF:(h + 1) * HALF] = rows[:, qi * HALF:(qi + 1) * HALF]
    for qi in range(2):
        wide = grad_t[qi].astype(F32)
        delta[qi] = jnp.sum(wide * att_t[qi].astype(F32), axis=0, keepdims=True)
        grad[qi] = wide.T.astype(BF16)

    def backward(yy, df):
        df[...] = jnp.zeros_like(df)

        def tile(t, carry):
            qi, ki = (t + 1) // 2, t // 2
            scores, keys, values, queries = tile_scores(yy, qi, ki)
            probs = jnp.exp2(scores - m_ref[qi])
            grad_probs = mm(values, grad_t[qi])
            grad_scores = (probs * (grad_probs - delta[qi])).astype(BF16)
            rows = pl.ds(pl.multiple_of(ki * HALF, HALF), HALF)
            grad_keys = mm(grad_scores, queries).reshape(4, HALF, HEAD_DIM)
            grad_values = mm(probs.astype(BF16), grad[qi]).reshape(4, HALF, HEAD_DIM)
            df[:, 0, rows, :] += grad_keys
            df[:, 1, rows, :] += grad_values
            dq_t[qi] += mm_tn(keys, grad_scores)
            return carry

        lax.fori_loop(0, 3, tile, 0)

    near = pl.ds(2 * xh, 2)
    over = pl.ds(2 * (1 - xh), 2)

    backward(y2, df)
    d_send[0, 0] = df[near].astype(BF16)
    d_far_right = copy(d_send.at[0, 0], d_rin2, y_right)
    d_send[0, 1] = df[over].astype(BF16)
    d_far_left = copy(d_send.at[0, 1], d_lin2, y_left)
    long_1 = out_hop(1, True, long_0)

    arrived(gw_over[0])
    gw_send[0] = (gw_term(xh, y2) + gw_xin[0].astype(F32)).astype(BF16)
    gw_far = (
        copy(gw_send.at[0, pl.ds(0, 160)], gw_rin2, y_right),
        copy(gw_send.at[0, pl.ds(160, 160)], gw_lin2, y_left),
    )

    backward(yr, df_right)
    d_send[1, 1] = df_right[over].astype(BF16)
    d_right = [copy(d_send.at[1, 1], d_rin.at[1], y_right)]
    backward(yl, df)
    short_2 = out_hop(2, False, short_1)
    arrived(d_far_left)
    d_send[2, 1] = (df[over] + d_lin2[...].astype(F32)).astype(BF16)
    d_left = [copy(d_send.at[2, 1], d_lin.at[1], y_left)]
    arrived(d_far_right)
    d_send[1, 0] = (df_right[near] + d_rin2[...].astype(F32)).astype(BF16)
    d_right.append(copy(d_send.at[1, 0], d_rin.at[0], y_right))
    d_send[2, 0] = df[near].astype(BF16)
    d_left.append(copy(d_send.at[2, 0], d_lin.at[0], y_left))
    long_2 = out_hop(2, True, long_1)

    arrived(*gw_far)
    arrived(*gw_over[1:])
    low, high = pl.ds(0, 160), pl.ds(160, 160)
    term = gw_term(xh, yr) + gw_xin[1].astype(F32)
    gw_send[1, low] = (term[:160] + gw_rin2[...].astype(F32)).astype(BF16)
    gw_send[1, high] = term[160:].astype(BF16)
    term = gw_term(xh, yl) + gw_xin[2].astype(F32)
    gw_send[2, low] = term[:160].astype(BF16)
    gw_send[2, high] = (term[160:] + gw_lin2[...].astype(F32)).astype(BF16)
    gw_near = (copy(gw_send.at[1], gw_rin, y_right), copy(gw_send.at[2], gw_lin, y_left))

    backward(y, df)
    short_3 = out_hop(3, False, short_2)
    for qi in range(2):
        for h in range(2):
            dq_b[h, pl.ds(qi * HALF, HALF), :] = dq_t[qi, :, h * HALF:(h + 1) * HALF].T * SCALE
    dq_core = copy(dq_b.at[p], dq_in, core_peer)
    long_3 = out_hop(3, True, long_2)

    arrived(d_right[0], d_left[0])
    d_send[3, 1] = (df[over] + d_rin[1].astype(F32) + d_lin[1].astype(F32)).astype(BF16)
    sem_d = take(2)
    d_over = [
        pltpu.make_async_remote_copy(
            src_ref=d_send.at[3, 1, h], dst_ref=d_x.at[c], send_sem=ss.at[sem_d + i],
            recv_sem=rs.at[sem_d + i], device_id=to, device_id_type=MESH,
        )
        for i, (h, to) in enumerate(((c, xh_peer), (p, xh_cross)))
    ]
    for d in d_over:
        d.start()
    sent.extend(d_over)

    first = c == 0

    def place(ref, mine, theirs):
        ref[:, :HEAD_DIM] = jnp.where(first, mine, theirs)
        ref[:, HEAD_DIM:] = jnp.where(first, theirs, mine)

    arrived(dq_core)
    place(dq_ref, dq_b[c], dq_in[...])
    store(1, dq_ref, dq_hbm)

    arrived(*short_3)
    for h in range(2):
        out_fin[h] = out_term(z, h) + out_in[1 - h, 3, h].astype(F32)
    gw_ref[...] = gw_term(xh, y) + gw_xin[3].astype(F32)

    arrived(d_right[1], d_left[1])
    for part in range(2):
        total = df[near, part] + d_rin[0, :, part].astype(F32) + d_lin[0, :, part].astype(F32)
        fin[:, part] = total
    fin_core = copy(fin.at[p], fin_in, core_peer)

    arrived(*long_3)
    for h in range(2):
        out_send[0, 4, h] = (out_fin[h] + out_in[h, 3, h].astype(F32)).astype(BF16)
    pair_ici, pair_core = take(2), take()
    to_peers = [
        pltpu.make_async_remote_copy(
            src_ref=out_send.at[0, 4, h], dst_ref=out_pair_ici, send_sem=ss.at[pair_ici + h],
            recv_sem=rs.at[pair_ici], device_id=xl_peers[h], device_id_type=MESH,
        )
        for h in range(2)
    ]
    to_core = pltpu.make_async_remote_copy(
        src_ref=out_send.at[0, 4, p], dst_ref=out_pair_core, send_sem=ss.at[pair_core],
        recv_sem=rs.at[pair_core], device_id=core_peer, device_id_type=MESH,
    )

    @pl.when(same)
    def _():
        to_core.start()

    @pl.when(jnp.logical_not(same))
    def _():
        to_peers[0].start()
        to_peers[1].start()

    arrived(*gw_near)
    gw_ref[...] += gw_rin[...].astype(F32) + gw_lin[...].astype(F32)
    store(4, gw_ref, gw_hbm)

    arrived(fin_core, *d_over)
    for i, (ref, factor) in enumerate(((dk_ref, SCALE), (dv_ref, 1.0))):
        mine = (fin[c, i] + d_x[c, i].astype(F32)) * factor
        theirs = (fin_in[i] + d_x[p, i].astype(F32)) * factor
        place(ref, mine, theirs)
        store(2 + i, ref, (dk_hbm, dv_hbm)[i])

    arrived(to_peers[0])

    @pl.when(same)
    def _():
        out_ref[...] = out_send[0, 4, c].astype(F32) + out_pair_ici[...].astype(F32)
        to_core.wait_send()

    @pl.when(jnp.logical_not(same))
    def _():
        to_core.wait_recv()
        out_ref[...] = out_pair_core[...].astype(F32) + out_pair_ici[...].astype(F32)
        to_peers[0].wait_send()
        to_peers[1].wait_send()
        cot_core.wait_send()
        for pair in cot_own:
            for d in pair:
                d.wait_send()

    cot_ici.wait_send()
    cot_lead.wait_send()
    cot_trail.wait_send()

    store(0, out_ref, out_hbm)
    for d in sent:
        d.wait_send()
    for d in stores:
        d.wait()
    assert used[0] <= SEMS, used[0]


def fused(pos, q, k, v, w, ct):
    vm = pltpu.VMEM
    scratch = [
        vm((16, 2 * TOKENS + 16, HEAD_DIM), BF16),
        vm((16, HEAD_DIM), BF16),
        vm((2, TOKENS, HEAD_DIM), BF16),
        vm((8, COLS, FEATS), BF16),
        vm((8, 2, COLS, TOKENS), BF16),
        vm((2, 1, TOKENS), F32),
        vm((2, 1, TOKENS), F32),
        vm((2, HEAD_DIM, TOKENS), F32),
        vm((2, HEAD_DIM, TOKENS), BF16),
        vm((2, 2, TOKENS, HEAD_DIM), BF16),
        vm((2, TOKENS, FEATS), BF16),
        vm((2, 2, HEAD_DIM, TOKENS), F32),
        vm((2, HEAD_DIM, TOKENS), F32),
        vm((2, HEAD_DIM, TOKENS), BF16),
        vm((2, TOKENS, HEAD_DIM), BF16),
        vm((2, 1, TOKENS), F32),
        vm((2, 5, 2, COLS, TOKENS), BF16),
        vm((2, 4, 2, COLS, TOKENS), BF16),
        vm((2, COLS, TOKENS), F32),
        vm((COLS, TOKENS), BF16),
        vm((COLS, TOKENS), BF16),
        vm((4, COLS, FEATS), BF16),
        vm((4, COLS, FEATS), BF16),
        vm((3, COLS, FEATS), BF16),
        vm((COLS // 2, FEATS), BF16),
        vm((COLS // 2, FEATS), BF16),
        vm((COLS, FEATS), BF16),
        vm((COLS, FEATS), BF16),
        vm((4, 2, TOKENS, HEAD_DIM), F32),
        vm((4, 2, TOKENS, HEAD_DIM), F32),
        vm((4, 2, 2, 2, TOKENS, HEAD_DIM), BF16),
        vm((2, 2, TOKENS, HEAD_DIM), BF16),
        vm((2, 2, TOKENS, HEAD_DIM), BF16),
        vm((2, 2, 2, TOKENS, HEAD_DIM), BF16),
        vm((2, 2, 2, TOKENS, HEAD_DIM), BF16),
        vm((2, 2, TOKENS, HEAD_DIM), BF16),
        vm((2, 2, TOKENS, HEAD_DIM), F32),
        vm((2, TOKENS, HEAD_DIM), F32),
        vm((2, HEAD_DIM, TOKENS), F32),
        vm((2, TOKENS, HEAD_DIM), F32),
        vm((TOKENS, HEAD_DIM), F32),
        pltpu.SemaphoreType.DMA((SEMS,)),
        pltpu.SemaphoreType.DMA((SEMS,)),
        pltpu.SemaphoreType.DMA((10,)),
    ]
    in_hbm = pl.BlockSpec(memory_space=pl.ANY)
    return pl.pallas_call(
        kernel,
        name="attention_core",
        out_shape=OUT_SHAPES,
        in_specs=[pl.BlockSpec(memory_space=pltpu.SMEM)] + [in_hbm] * 5,
        out_specs=(in_hbm,) * 5,
        scratch_shapes=[vm(d.shape, d.dtype) for d in OUT_SHAPES] + scratch,
        compiler_params=pltpu.CompilerParams(
            collective_id=0, has_side_effects=True, vmem_limit_bytes=62 << 20
        ),
    )(pos, q, k, v, w, ct)


OUT_SHAPES = (
    jax.ShapeDtypeStruct((COLS, TOKENS), F32),
    jax.ShapeDtypeStruct((TOKENS, FEATS), F32),
    jax.ShapeDtypeStruct((TOKENS, FEATS), F32),
    jax.ShapeDtypeStruct((TOKENS, FEATS), F32),
    jax.ShapeDtypeStruct((COLS, FEATS), F32),
)


def store_kernel(*refs):
    results, outs, held, sems = refs[:5], refs[5:10], refs[10:15], refs[15]
    loads = [pltpu.make_async_copy(results[i], held[i], sems.at[0, i]) for i in range(5)]
    stores = [pltpu.make_async_copy(held[i], outs[i], sems.at[1, i]) for i in range(5)]
    for d in loads:
        d.start()
    for load, store in zip(loads, stores):
        load.wait()
        store.start()
    for d in stores:
        d.wait()


def stored(*results):
    return pl.pallas_call(
        store_kernel,
        name="store_results",
        out_shape=OUT_SHAPES,
        in_specs=[pl.BlockSpec(memory_space=pl.ANY)] * 5,
        out_specs=(pl.BlockSpec(memory_space=pl.ANY),) * 5,
        scratch_shapes=[pltpu.VMEM(d.shape, d.dtype) for d in OUT_SHAPES]
        + [pltpu.SemaphoreType.DMA((2, 5))],
        compiler_params=pltpu.CompilerParams(vmem_limit_bytes=62 << 20),
    )(*results)


def shards(query_states, key_states, value_states, positions, out_weight, cotangent):
    results = fused(
        positions, query_states, key_states, value_states, out_weight.T, cotangent.T
    )
    out_t, grad_queries, grad_keys, grad_values, gw_t = stored(*results)
    return out_t.T, grad_queries, grad_keys, grad_values, gw_t.T


def solution(mesh):
    in_specs = (
        P("seq", "fsdp"),
        P("seq", "fsdp"),
        P("seq", "fsdp"),
        P("seq"),
        P("fsdp", "seq"),
        P("seq", "fsdp"),
    )
    out_specs = (
        P("seq", "fsdp"),
        P("seq", "fsdp"),
        P("seq", "fsdp"),
        P("seq", "fsdp"),
        P("fsdp", "seq"),
    )
    return jax.shard_map(shards, mesh=mesh, in_specs=in_specs, out_specs=out_specs, check_vma=False)
```

```python
import math

import jax
import jax.numpy as jnp
from jax import lax
from jax.experimental import pallas as pl
from jax.experimental.pallas import tpu as pltpu
from jax.sharding import PartitionSpec as P

HEAD_DIM = 128
TOKENS = 256
HALF = 128
COLS = 320
FEATS = 256
MESH = pl.DeviceIdType.MESH
BF16 = jnp.bfloat16
F32 = jnp.float32
SCALE = HEAD_DIM ** (-0.5)
SCALE_LOG2 = SCALE * math.log2(math.e)
BLOCKED = -1e30
SEMS = 112


def mm(a, b):
    return jnp.dot(a, b, preferred_element_type=F32)


def mm_nt(a, b):
    return lax.dot_general(a, b, (((1,), (1,)), ((), ())), preferred_element_type=F32)


def mm_tn(a, b):
    return lax.dot_general(a, b, (((0,), (0,)), ((), ())), preferred_element_type=F32)


def kernel(
    pos_ref, q_ref, k_ref, v_ref, w_ref, ct_ref,
    out_hbm, dq_hbm, dk_hbm, dv_hbm, gw_hbm,
    out_ref, dq_ref, dk_ref, dv_ref, gw_ref,
    kvr, res, qt, wt, cot,
    m_ref, l_ref, acc, att_t, att, att_full,
    pga, pga_in, grad_t, grad, delta,
    out_send, out_in, out_fin, out_pair_ici, out_pair_core,
    gw_xsend, gw_xin, gw_send, gw_rin2, gw_lin2, gw_rin, gw_lin,
    df, df_right, d_send, d_rin2, d_lin2, d_rin, d_lin, d_x, fin, fin_in,
    dq_t, dq_b, dq_in,
    ss, rs, ls,
):
    seq = lax.axis_index("seq")
    fsdp = lax.axis_index("fsdp")
    xh, y, c = seq // 8, (seq // 2) % 4, seq % 2
    z, xl = fsdp // 2, fsdp % 2
    p = 1 - c
    same = c == xl

    def dev(xh_, y_, c_, z_, xl_):
        return (xh_ * 8 + y_ * 2 + c_, z_ * 2 + xl_)

    yr, yl, y2 = (y + 1) % 4, (y + 3) % 4, (y + 2) % 4
    zr, zl = (z + 1) % 8, (z + 7) % 8
    core_peer = dev(xh, y, p, z, xl)
    xh_peer = dev(1 - xh, y, c, z, xl)
    y_right, y_left = dev(xh, yr, c, z, xl), dev(xh, yl, c, z, xl)
    z_right, z_left = dev(xh, y, c, zr, xl), dev(xh, y, c, zl, xl)
    xl_peers = [dev(xh, y, h, z, 1 - xl) for h in range(2)]
    xl_owner = dev(xh, y, xl, z, 1 - xl)

    used = [0]
    sent = []

    def take(count=1):
        first = used[0]
        used[0] += count
        return first

    def copy(src, dst, to):
        i = take()
        d = pltpu.make_async_remote_copy(
            src_ref=src, dst_ref=dst, send_sem=ss.at[i], recv_sem=rs.at[i],
            device_id=to, device_id_type=MESH,
        )
        d.start()
        sent.append(d)
        return d

    stores = []

    def store(i, src, dst):
        d = pltpu.make_async_copy(src, dst, ls.at[5 + i])
        d.start()
        stores.append(d)

    def arrived(*copies):
        for d in copies:
            d.wait_recv()

    own = y * 4 + xh * 2
    w_own = y * 2 + xh
    mine = pl.ds(pl.multiple_of(c * HEAD_DIM, HEAD_DIM), HEAD_DIM)
    other = pl.ds(pl.multiple_of(p * HEAD_DIM, HEAD_DIM), HEAD_DIM)
    key_rows, value_rows, res_rows = pl.ds(0, TOKENS), pl.ds(TOKENS, TOKENS), pl.ds(2 * TOKENS, 16)
    key_copy = pltpu.make_async_copy(k_ref.at[:, mine], kvr.at[own + c, key_rows], ls.at[0])
    value_copy = pltpu.make_async_copy(v_ref.at[:, mine], kvr.at[own + c, value_rows], ls.at[1])
    query_copy = pltpu.make_async_copy(q_ref.at[:, mine], qt.at[c], ls.at[2])
    weight_copy = pltpu.make_async_copy(w_ref, wt.at[w_own], ls.at[3])
    cot_copy = pltpu.make_async_copy(ct_ref, cot.at[z, c], ls.at[4])
    key_copy.start()
    value_copy.start()

    @pl.when(same)
    def _():
        cot_copy.start()

    query_copy.start()
    weight_copy.start()

    barrier = pltpu.get_barrier_semaphore()
    z_cross = [dev(xh, y, p, zr, xl), dev(xh, y, p, zl, xl)]
    xh_cross = dev(1 - xh, y, p, z, xl)
    peers = [core_peer, xh_peer, y_right, y_left, z_right, z_left] + xl_peers + z_cross + [xh_cross]
    for peer in peers:
        pl.semaphore_signal(barrier, inc=1, device_id=peer, device_id_type=MESH)
    residue = jnp.full((16, HEAD_DIM), (pos_ref[0] % 16).astype(F32)).astype(BF16)
    res[...] = residue
    kvr[own + c, res_rows, :] = residue
    key_copy.wait()
    value_copy.wait()
    pl.semaphore_wait(barrier, len(peers))

    sem_ici, sem_core, sem_z = take(2), take(), take(4)
    z_lead = dev(xh, y, xl, jnp.where(c == 0, zr, zl), xl)
    z_trail = dev(xh, y, xl, jnp.where(c == 0, zl, zr), xl)

    def cot_copy_to(h, src, to, send, recv):
        return pltpu.make_async_remote_copy(
            src_ref=src, dst_ref=cot.at[z, h], send_sem=ss.at[send], recv_sem=rs.at[recv],
            device_id=to, device_id_type=MESH,
        )

    cot_ici = cot_copy_to(c, ct_ref, xl_owner, sem_ici, sem_ici + c)
    cot_core = cot_copy_to(c, ct_ref, core_peer, sem_core, sem_core)
    cot_lead = cot_copy_to(c, ct_ref, z_lead, sem_z, sem_z + 3 * c)
    cot_trail = cot_copy_to(c, ct_ref, z_trail, sem_z + 1, sem_z + 2 - c)
    sem_own = take(4)
    cot_own = [
        [
            cot_copy_to(h, cot.at[z, h], to, sem_own + 2 * side + h, sem_z + 2 * side + h)
            for side, to in enumerate((z_right, z_left))
        ]
        for h in range(2)
    ]
    cot_ici.start()

    core_first = (
        copy(k_ref.at[:, other], kvr.at[own + c, key_rows], core_peer),
        copy(v_ref.at[:, other], kvr.at[own + c, value_rows], core_peer),
        copy(res, kvr.at[own + c, res_rows], core_peer),
    )

    def kv_send(slot, *targets):
        block = kvr.at[slot]
        return [copy(block, block, to) for to in targets]

    kv_c = kv_send(own + c, y_right, y_left, xh_peer)
    cot_lead.start()

    @pl.when(jnp.logical_not(same))
    def _():
        cot_core.start()

    w_right = copy(w_ref, wt.at[w_own], y_right)
    w_left = copy(w_ref, wt.at[w_own], y_left)
    q_core = copy(q_ref.at[:, other], qt.at[c], core_peer)

    def z_pair(right_slot, left_slot, lead):
        a = cot.at[right_slot % 8, 0 if lead else 1]
        b = cot.at[left_slot % 8, 1 if lead else 0]
        return copy(a, a, z_right), copy(b, b, z_left)

    arrived(*core_first)
    kv_p = kv_send(own + p, y_right, y_left, xh_peer)
    cot_trail.start()

    @pl.when(same)
    def _():
        cot_copy.wait()
        cot_core.wait_recv()

    @pl.when(jnp.logical_not(same))
    def _():
        for h in range(2):
            cot_copy_to(h, ct_ref, xl_owner, sem_ici, sem_ici + h).wait_recv()
        cot_own[0][0].start()
        cot_own[1][1].start()

    w_xh = [copy(w_ref, wt.at[w_own], xh_peer)]

    acc[...] = jnp.zeros_like(acc)
    l_ref[...] = jnp.zeros_like(l_ref)
    m_ref[...] = jnp.full_like(m_ref, BLOCKED)
    pga[...] = jnp.zeros_like(pga)
    dq_t[...] = jnp.zeros_like(dq_t)
    query_copy.wait()
    weight_copy.wait()
    arrived(q_core)

    kv_far = []
    over_own = y * 4 + (1 - xh) * 2

    arrived(kv_c[0])
    kv_far += kv_send(yl * 4 + xh * 2 + c, y_right)
    arrived(kv_c[1], kv_c[2])
    kv_over_c = kv_send(over_own + c, y_right, y_left)

    @pl.when(jnp.logical_not(same))
    def _():
        cot_own[1][0].start()
        cot_own[0][1].start()

    arrived(cot_own[0][0], cot_own[1][1])
    z_lead_two = z_pair(z + 7, z + 1, True)
    arrived(w_right, w_left)
    w_low, w_high = wt.at[yl * 2 + xh, pl.ds(0, 160)], wt.at[yr * 2 + xh, pl.ds(160, 160)]
    w_far = (copy(w_low, w_low, y_right), copy(w_high, w_high, y_left))
    w_xh.append(copy(wt.at[yl * 2 + xh], wt.at[yl * 2 + xh], xh_peer))
    w_xh.append(copy(wt.at[yr * 2 + xh], wt.at[yr * 2 + xh], xh_peer))
    arrived(cot_own[1][0], cot_own[0][1])
    z_trail_two = z_pair(z + 7, z + 1, False)
    arrived(*kv_p)
    kv_over_p = kv_send(over_own + p, y_right, y_left)
    kv_far += kv_send(yr * 4 + xh * 2 + p, y_left)

    ahead = (
        lax.broadcasted_iota(jnp.int32, (1, HALF, TOKENS), 2) % HALF
        - lax.broadcasted_iota(jnp.int32, (1, HALF, TOKENS), 1)
    )

    def residue_rows(slot, count):
        return kvr[pl.ds(slot, count), pl.ds(2 * TOKENS, 16), :].astype(F32)[:, 0:1, :]

    query_res = residue_rows(own, 2)
    query_res = jnp.concatenate([query_res[0:1], query_res[1:2]], axis=2)

    def tile_scores(yy, qi, ki):
        key_res = residue_rows(yy * 4, 4)
        key_res = jnp.concatenate([key_res, key_res], axis=2)
        bound = jnp.where(key_res <= query_res, 0, 1) - jnp.where(qi > ki, 4 * HALF, 0)
        rows = pl.multiple_of(ki * HALF, HALF)
        keys = kvr[pl.ds(yy * 4, 4), pl.ds(rows, HALF), :].reshape(4 * HALF, HEAD_DIM)
        values = kvr[pl.ds(yy * 4, 4), pl.ds(TOKENS + rows, HALF), :].reshape(4 * HALF, HEAD_DIM)
        query_rows = pl.ds(pl.multiple_of(qi * HALF, HALF), HALF)
        queries = qt[:, query_rows, :].reshape(TOKENS, HEAD_DIM)
        scores = mm_nt(keys, queries) * SCALE_LOG2
        seen = ahead >= bound
        scores = jnp.where(seen, scores.reshape(4, HALF, TOKENS), BLOCKED)
        return scores.reshape(4 * HALF, TOKENS), keys, values, queries

    def forward(yy):
        def tile(t, carry):
            qi, ki = (t + 1) // 2, t // 2
            scores, _, values, _ = tile_scores(yy, qi, ki)
            old = m_ref[qi]
            new = jnp.maximum(old, jnp.max(scores, axis=0, keepdims=True))
            probs = jnp.exp2(scores - new)
            shrink = jnp.exp2(old - new)
            m_ref[qi] = new
            l_ref[qi] = l_ref[qi] * shrink + jnp.sum(probs, axis=0, keepdims=True)
            acc[qi] = acc[qi] * shrink + mm_tn(values, probs.astype(BF16))
            return carry

        lax.fori_loop(0, 3, tile, 0)

    forward(y)
    arrived(*z_lead_two)
    z_lead_three = z_pair(z + 6, z + 2, True)
    arrived(*kv_over_c)
    kv_far += kv_send(yl * 4 + (1 - xh) * 2 + c, y_right)
    arrived(*w_far)
    w_xh.append(copy(wt.at[y2 * 2 + xh], wt.at[y2 * 2 + xh], xh_peer))
    arrived(*z_trail_two)
    z_trail_three = z_pair(z + 6, z + 2, False)
    arrived(*kv_over_p)
    kv_far += kv_send(yr * 4 + (1 - xh) * 2 + p, y_left)
    forward(yl)
    arrived(*z_lead_three)
    z_four = z_pair(z + 5, z + 3, True)
    forward(yr)
    arrived(*kv_far)
    forward(y2)

    for qi in range(2):
        total = l_ref[qi]
        rows = (acc[qi] / total).astype(BF16)
        att_t[qi] = rows
        m_ref[qi] = m_ref[qi] + jnp.log2(total)
        wide = rows.astype(F32)
        for h in range(2):
            att[c, h, pl.ds(qi * HALF, HALF), :] = wide[:, h * HALF:(h + 1) * HALF].T.astype(BF16)
    att_core = copy(att.at[c], att.at[c], core_peer)
    arrived(*w_xh)
    arrived(*z_trail_three)

    def w_block(i):
        return wt[(i % 4) * 2 + i // 4]

    def width_step(k, carry):
        i = (z + 5 + k) % 8
        weight = w_block(i)
        for h in range(2):
            term = mm_tn(weight, cot[i, h])
            pga[0, h] += term[:HEAD_DIM]
            pga[1, h] += term[HEAD_DIM:]
        return carry

    lax.fori_loop(0, 7, width_step, 0)
    arrived(att_core)
    for h in range(2):
        att_full[h] = jnp.concatenate([att[0, h], att[1, h]], axis=1)

    def out_term(i, h):
        return mm_nt(w_block(i), att_full[h])

    def out_hop(step, long_chain, got):
        sends = []
        halves = (0, 1) if long_chain else (1, 0)
        targets = ((z + 4 - step) % 8, (z + 4 + step) % 8)
        terms = [out_term(targets[side], halves[side]) for side in range(2)]
        for side, h in enumerate(halves):
            term = terms[side]
            if got is not None:
                arrived(got[side])
                term = term + out_in[side, step - 1, h].astype(F32)
            out_send[side, step, h] = term.astype(BF16)
            sends.append(
                copy(out_send.at[side, step, h], out_in.at[side, step, h], z_left if side else z_right)
            )
        return sends

    long_0 = out_hop(0, True, None)
    arrived(*z_four)

    width_step(7, 0)
    pga_core = copy(pga.at[p], pga_in, core_peer)

    def gw_term(x, yy):
        i = x * 4 + yy
        return mm(cot[i, 0], att_full[0]) + mm(cot[i, 1], att_full[1])

    gw_over = []
    for i, yy in enumerate((y2, yr, yl, y)):
        gw_xsend[i] = gw_term(1 - xh, yy).astype(BF16)
        gw_over.append(copy(gw_xsend.at[i], gw_xin.at[i], xh_peer))

    short_1 = out_hop(1, False, None)
    arrived(pga_core)
    for h in range(2):
        rows = (pga[c, h] + pga_in[h]).astype(BF16)
        for qi in range(2):
            grad_t[qi, :, h * HALF:(h + 1) * HALF] = rows[:, qi * HALF:(qi + 1) * HALF]
    for qi in range(2):
        wide = grad_t[qi].astype(F32)
        delta[qi] = jnp.sum(wide * att_t[qi].astype(F32), axis=0, keepdims=True)
        grad[qi] = wide.T.astype(BF16)

    def backward(yy, df):
        df[...] = jnp.zeros_like(df)

        def tile(t, carry):
            qi, ki = (t + 1) // 2, t // 2
            scores, keys, values, queries = tile_scores(yy, qi, ki)
            probs = jnp.exp2(scores - m_ref[qi])
            grad_probs = mm(values, grad_t[qi])
            grad_scores = (probs * (grad_probs - delta[qi])).astype(BF16)
            rows = pl.ds(pl.multiple_of(ki * HALF, HALF), HALF)
            grad_keys = mm(grad_scores, queries).reshape(4, HALF, HEAD_DIM)
            grad_values = mm(probs.astype(BF16), grad[qi]).reshape(4, HALF, HEAD_DIM)
            df[:, 0, rows, :] += grad_keys
            df[:, 1, rows, :] += grad_values
            dq_t[qi] += mm_tn(keys, grad_scores)
            return carry

        lax.fori_loop(0, 3, tile, 0)

    near = pl.ds(2 * xh, 2)
    over = pl.ds(2 * (1 - xh), 2)

    backward(y2, df)
    d_send[0, 0] = df[near].astype(BF16)
    d_far_right = copy(d_send.at[0, 0], d_rin2, y_right)
    d_send[0, 1] = df[over].astype(BF16)
    d_far_left = copy(d_send.at[0, 1], d_lin2, y_left)
    long_1 = out_hop(1, True, long_0)

    arrived(gw_over[0])
    gw_send[0] = (gw_term(xh, y2) + gw_xin[0].astype(F32)).astype(BF16)
    gw_far = (
        copy(gw_send.at[0, pl.ds(0, 160)], gw_rin2, y_right),
        copy(gw_send.at[0, pl.ds(160, 160)], gw_lin2, y_left),
    )

    backward(yr, df_right)
    d_send[1, 1] = df_right[over].astype(BF16)
    d_right = [copy(d_send.at[1, 1], d_rin.at[1], y_right)]
    short_2 = out_hop(2, False, short_1)
    backward(yl, df)
    arrived(d_far_left)
    d_send[2, 1] = (df[over] + d_lin2[...].astype(F32)).astype(BF16)
    d_left = [copy(d_send.at[2, 1], d_lin.at[1], y_left)]
    arrived(d_far_right)
    d_send[1, 0] = (df_right[near] + d_rin2[...].astype(F32)).astype(BF16)
    d_right.append(copy(d_send.at[1, 0], d_rin.at[0], y_right))
    d_send[2, 0] = df[near].astype(BF16)
    d_left.append(copy(d_send.at[2, 0], d_lin.at[0], y_left))
    long_2 = out_hop(2, True, long_1)

    arrived(*gw_far)
    arrived(*gw_over[1:])
    low, high = pl.ds(0, 160), pl.ds(160, 160)
    term = gw_term(xh, yr) + gw_xin[1].astype(F32)
    gw_send[1, low] = (term[:160] + gw_rin2[...].astype(F32)).astype(BF16)
    gw_send[1, high] = term[160:].astype(BF16)
    term = gw_term(xh, yl) + gw_xin[2].astype(F32)
    gw_send[2, low] = term[:160].astype(BF16)
    gw_send[2, high] = (term[160:] + gw_lin2[...].astype(F32)).astype(BF16)
    gw_near = (copy(gw_send.at[1], gw_rin, y_right), copy(gw_send.at[2], gw_lin, y_left))

    backward(y, df)
    short_3 = out_hop(3, False, short_2)
    for qi in range(2):
        for h in range(2):
            dq_b[h, pl.ds(qi * HALF, HALF), :] = dq_t[qi, :, h * HALF:(h + 1) * HALF].T * SCALE
    dq_core = copy(dq_b.at[p], dq_in, core_peer)
    long_3 = out_hop(3, True, long_2)

    arrived(d_right[0], d_left[0])
    d_send[3, 1] = (df[over] + d_rin[1].astype(F32) + d_lin[1].astype(F32)).astype(BF16)
    sem_d = take(2)
    d_over = [
        pltpu.make_async_remote_copy(
            src_ref=d_send.at[3, 1, h], dst_ref=d_x.at[c], send_sem=ss.at[sem_d + i],
            recv_sem=rs.at[sem_d + i], device_id=to, device_id_type=MESH,
        )
        for i, (h, to) in enumerate(((c, xh_peer), (p, xh_cross)))
    ]
    for d in d_over:
        d.start()
    sent.extend(d_over)

    first = c == 0

    def place(ref, mine, theirs):
        ref[:, :HEAD_DIM] = jnp.where(first, mine, theirs)
        ref[:, HEAD_DIM:] = jnp.where(first, theirs, mine)

    arrived(dq_core)
    place(dq_ref, dq_b[c], dq_in[...])
    store(1, dq_ref, dq_hbm)

    arrived(*short_3)
    for h in range(2):
        out_fin[h] = out_term(z, h) + out_in[1 - h, 3, h].astype(F32)
    gw_ref[...] = gw_term(xh, y) + gw_xin[3].astype(F32)

    arrived(d_right[1], d_left[1])
    for part in range(2):
        total = df[near, part] + d_rin[0, :, part].astype(F32) + d_lin[0, :, part].astype(F32)
        fin[:, part] = total
    fin_core = copy(fin.at[p], fin_in, core_peer)

    arrived(*long_3)
    for h in range(2):
        out_send[0, 4, h] = (out_fin[h] + out_in[h, 3, h].astype(F32)).astype(BF16)
    pair_ici, pair_core = take(2), take()
    to_peers = [
        pltpu.make_async_remote_copy(
            src_ref=out_send.at[0, 4, h], dst_ref=out_pair_ici, send_sem=ss.at[pair_ici + h],
            recv_sem=rs.at[pair_ici], device_id=xl_peers[h], device_id_type=MESH,
        )
        for h in range(2)
    ]
    to_core = pltpu.make_async_remote_copy(
        src_ref=out_send.at[0, 4, p], dst_ref=out_pair_core, send_sem=ss.at[pair_core],
        recv_sem=rs.at[pair_core], device_id=core_peer, device_id_type=MESH,
    )

    @pl.when(same)
    def _():
        to_core.start()

    @pl.when(jnp.logical_not(same))
    def _():
        to_peers[0].start()
        to_peers[1].start()

    arrived(*gw_near)
    gw_ref[...] += gw_rin[...].astype(F32) + gw_lin[...].astype(F32)
    store(4, gw_ref, gw_hbm)

    arrived(fin_core, *d_over)
    for i, (ref, factor) in enumerate(((dk_ref, SCALE), (dv_ref, 1.0))):
        mine = (fin[c, i] + d_x[c, i].astype(F32)) * factor
        theirs = (fin_in[i] + d_x[p, i].astype(F32)) * factor
        place(ref, mine, theirs)
        store(2 + i, ref, (dk_hbm, dv_hbm)[i])

    arrived(to_peers[0])

    @pl.when(same)
    def _():
        out_ref[...] = out_send[0, 4, c].astype(F32) + out_pair_ici[...].astype(F32)
        to_core.wait_send()

    @pl.when(jnp.logical_not(same))
    def _():
        to_core.wait_recv()
        out_ref[...] = out_pair_core[...].astype(F32) + out_pair_ici[...].astype(F32)
        to_peers[0].wait_send()
        to_peers[1].wait_send()
        cot_core.wait_send()
        for pair in cot_own:
            for d in pair:
                d.wait_send()

    cot_ici.wait_send()
    cot_lead.wait_send()
    cot_trail.wait_send()

    store(0, out_ref, out_hbm)
    for d in sent:
        d.wait_send()
    for d in stores:
        d.wait()
    assert used[0] <= SEMS, used[0]


def fused(pos, q, k, v, w, ct):
    vm = pltpu.VMEM
    scratch = [
        vm((16, 2 * TOKENS + 16, HEAD_DIM), BF16),
        vm((16, HEAD_DIM), BF16),
        vm((2, TOKENS, HEAD_DIM), BF16),
        vm((8, COLS, FEATS), BF16),
        vm((8, 2, COLS, TOKENS), BF16),
        vm((2, 1, TOKENS), F32),
        vm((2, 1, TOKENS), F32),
        vm((2, HEAD_DIM, TOKENS), F32),
        vm((2, HEAD_DIM, TOKENS), BF16),
        vm((2, 2, TOKENS, HEAD_DIM), BF16),
        vm((2, TOKENS, FEATS), BF16),
        vm((2, 2, HEAD_DIM, TOKENS), F32),
        vm((2, HEAD_DIM, TOKENS), F32),
        vm((2, HEAD_DIM, TOKENS), BF16),
        vm((2, TOKENS, HEAD_DIM), BF16),
        vm((2, 1, TOKENS), F32),
        vm((2, 5, 2, COLS, TOKENS), BF16),
        vm((2, 4, 2, COLS, TOKENS), BF16),
        vm((2, COLS, TOKENS), F32),
        vm((COLS, TOKENS), BF16),
        vm((COLS, TOKENS), BF16),
        vm((4, COLS, FEATS), BF16),
        vm((4, COLS, FEATS), BF16),
        vm((3, COLS, FEATS), BF16),
        vm((COLS // 2, FEATS), BF16),
        vm((COLS // 2, FEATS), BF16),
        vm((COLS, FEATS), BF16),
        vm((COLS, FEATS), BF16),
        vm((4, 2, TOKENS, HEAD_DIM), F32),
        vm((4, 2, TOKENS, HEAD_DIM), F32),
        vm((4, 2, 2, 2, TOKENS, HEAD_DIM), BF16),
        vm((2, 2, TOKENS, HEAD_DIM), BF16),
        vm((2, 2, TOKENS, HEAD_DIM), BF16),
        vm((2, 2, 2, TOKENS, HEAD_DIM), BF16),
        vm((2, 2, 2, TOKENS, HEAD_DIM), BF16),
        vm((2, 2, TOKENS, HEAD_DIM), BF16),
        vm((2, 2, TOKENS, HEAD_DIM), F32),
        vm((2, TOKENS, HEAD_DIM), F32),
        vm((2, HEAD_DIM, TOKENS), F32),
        vm((2, TOKENS, HEAD_DIM), F32),
        vm((TOKENS, HEAD_DIM), F32),
        pltpu.SemaphoreType.DMA((SEMS,)),
        pltpu.SemaphoreType.DMA((SEMS,)),
        pltpu.SemaphoreType.DMA((10,)),
    ]
    in_hbm = pl.BlockSpec(memory_space=pl.ANY)
    return pl.pallas_call(
        kernel,
        name="attention_core",
        out_shape=OUT_SHAPES,
        in_specs=[pl.BlockSpec(memory_space=pltpu.SMEM)] + [in_hbm] * 5,
        out_specs=(in_hbm,) * 5,
        scratch_shapes=[vm(d.shape, d.dtype) for d in OUT_SHAPES] + scratch,
        compiler_params=pltpu.CompilerParams(
            collective_id=0, has_side_effects=True, vmem_limit_bytes=62 << 20
        ),
    )(pos, q, k, v, w, ct)


OUT_SHAPES = (
    jax.ShapeDtypeStruct((COLS, TOKENS), F32),
    jax.ShapeDtypeStruct((TOKENS, FEATS), F32),
    jax.ShapeDtypeStruct((TOKENS, FEATS), F32),
    jax.ShapeDtypeStruct((TOKENS, FEATS), F32),
    jax.ShapeDtypeStruct((COLS, FEATS), F32),
)


def store_kernel(*refs):
    results, outs, held, sems = refs[:5], refs[5:10], refs[10:15], refs[15]
    loads = [pltpu.make_async_copy(results[i], held[i], sems.at[0, i]) for i in range(5)]
    stores = [pltpu.make_async_copy(held[i], outs[i], sems.at[1, i]) for i in range(5)]
    for d in loads:
        d.start()
    for load, store in zip(loads, stores):
        load.wait()
        store.start()
    for d in stores:
        d.wait()


def stored(*results):
    return pl.pallas_call(
        store_kernel,
        name="store_results",
        out_shape=OUT_SHAPES,
        in_specs=[pl.BlockSpec(memory_space=pl.ANY)] * 5,
        out_specs=(pl.BlockSpec(memory_space=pl.ANY),) * 5,
        scratch_shapes=[pltpu.VMEM(d.shape, d.dtype) for d in OUT_SHAPES]
        + [pltpu.SemaphoreType.DMA((2, 5))],
        compiler_params=pltpu.CompilerParams(vmem_limit_bytes=62 << 20),
    )(*results)


def shards(query_states, key_states, value_states, positions, out_weight, cotangent):
    results = fused(
        positions, query_states, key_states, value_states, out_weight.T, cotangent.T
    )
    out_t, grad_queries, grad_keys, grad_values, gw_t = stored(*results)
    return out_t.T, grad_queries, grad_keys, grad_values, gw_t.T


def solution(mesh):
    in_specs = (
        P("seq", "fsdp"),
        P("seq", "fsdp"),
        P("seq", "fsdp"),
        P("seq"),
        P("fsdp", "seq"),
        P("seq", "fsdp"),
    )
    out_specs = (
        P("seq", "fsdp"),
        P("seq", "fsdp"),
        P("seq", "fsdp"),
        P("seq", "fsdp"),
        P("fsdp", "seq"),
    )
    return jax.shard_map(shards, mesh=mesh, in_specs=in_specs, out_specs=out_specs, check_vma=False)
```
